512 devices in a mesh: rep: 8 (over z_lo), fsdp: 64 (over y, x, z_hi, core).
Axes of the slice: x: 4, y: 4, z: 16 (z_hi: 2, z_lo: 8; z = z_hi * 8 + z_lo), core: 2. Of those that a mesh axis runs over, the one named last changes fastest.
Arguments:
- inputs: bfloat16 [8, 8192, 7168], P('rep', 'fsdp'), may hold values from -6 to 6
- cotangent: bfloat16 [8, 8192, 7168], P('rep', 'fsdp'), may hold values from -6 to 6
- weights: float32 [8, 2, 3584, 128], P('rep', None, 'fsdp'), may hold values from -6 to 6
- first_moment: float32 [8, 2, 3584, 128], P('rep', None, 'fsdp'), may hold values from -0.015625 to 0.015625
- second_moment: float32 [8, 2, 3584, 128], P('rep', None, 'fsdp'), may hold values from 1e-08 to 1e-05
- anchor: float32 [3584, 128], P('fsdp'), may hold values from -6 to 6
- momentum: float32 [3584, 128], P('fsdp'), may hold values from -4 to 4
- fragment: int32 [1], replicated, may hold values from 1 to 64
Outputs:
- new_weights: float32 [8, 2, 3584, 128], P('rep', None, 'fsdp')
- new_anchor: float32 [3584, 128], P('fsdp')
- new_momentum: float32 [3584, 128], P('fsdp')
The draws below stay inside these ranges and needn't reach their ends.
All inputs are finite; a program needn't handle non-finite values.
Results may differ from the reference program's by a relative error of at most 0.0022.
Values may be sent and summed in bfloat16 or wider, within the bound.
A program may use at most 64 MiB of HBM per device.

```python
import math
import jax
import jax.numpy as jnp
from jax import lax

D = 7168
H = 32
L = 2
TOK_DEV = 128
TOKENS = 8192
FLAT = 3584
N_REP = 8
N_FSDP = 64


def block_levels(key, shape, pieces, low, largest):
    level, own = 1.0, jax.random.fold_in(key, 6)
    for axis_at, parts in pieces:
        draws = jnp.exp(jax.random.uniform(jax.random.fold_in(own, axis_at), (parts,), jnp.float32, low / len(pieces), largest / len(pieces)))
        level = level * jnp.repeat(draws, shape[axis_at] // parts).reshape([-1 if axis == axis_at else 1 for axis in range(len(shape))])
    return level


def normal_values(rng, extent, width, most, shards=(), kind=jnp.bfloat16):
    drawn = jax.random.normal(rng, extent, jnp.float32) * width
    if len(shards) > 0:
        drawn = block_levels(rng, extent, shards, -0.22, 0.18) * drawn
    return jnp.clip(drawn, min=-most, max=most).astype(kind)


def setup_inputs(seed: int = 0) -> dict:
    key_of = jax.random.split(jax.random.key(seed), 9)
    return {
        "inputs": normal_values(key_of[0], (N_REP, TOKENS, D), 1.0, 6.0, ((0, 8), (1, 64))),
        "cotangent": normal_values(key_of[1], (N_REP, TOKENS, D), 1.0, 6.0, ((0, 8), (1, 64))),
        "weights": normal_values(key_of[2], (N_REP, L, FLAT, 128), 1.0, 6.0, ((0, 8), (2, 64)), jnp.float32),
        "first_moment": normal_values(key_of[3], (N_REP, L, FLAT, 128), 0.001, 0.015625, ((0, 8), (2, 64)), jnp.float32),
        "second_moment": jnp.clip(jnp.exp(math.log(9.999999747378752e-06) - 6.9077553 * jax.random.uniform(key_of[4], (N_REP, L, FLAT, 128), jnp.float32) ** block_levels(key_of[4], (N_REP, L, FLAT, 128), ((0, 8), (2, 64)), -0.2, 0.2)), 9.99999993922529e-09, 9.999999747378752e-06),
        "anchor": normal_values(key_of[5], (FLAT, 128), 1.0, 6.0, ((0, 64),), jnp.float32),
        "momentum": normal_values(key_of[6], (FLAT, 128), 0.3, 4.0, ((0, 64),), jnp.float32),
        "fragment": jax.random.randint(key_of[7], (1,), 1, 65).astype(jnp.int32),
    }


norm_eps = 1e-05
beta_one = 0.9
beta_two = 0.95
adam_eps = 1e-08
decay_rate = 0.1
inner_rate = 0.05
outer_rate = 0.7
outer_beta = 0.9
mixing = 0.5

def layer_forward(hidden_in, w_in, w_out):
    inputs_f32 = hidden_in.astype(jnp.float32)
    inv_rms = lax.rsqrt(lax.optimization_barrier(jnp.mean(inputs_f32 * inputs_f32, axis=-1, keepdims=True)) + norm_eps)
    normed = (inputs_f32 * inv_rms).astype(jnp.bfloat16)
    in_scale = w_in.shape[1] ** (-0.5)
    out_scale = w_out.shape[0] ** (-0.5)
    pre_act = lax.dot_general(normed, w_in, (((1,), (1,)), ((), ())), preferred_element_type=jnp.float32) * in_scale
    activated = jax.nn.silu(pre_act).astype(jnp.bfloat16)
    layer_out = (inputs_f32 + jnp.dot(activated, w_out, preferred_element_type=jnp.float32) * out_scale).astype(jnp.bfloat16)
    return (layer_out, (inputs_f32, inv_rms, normed, pre_act, activated))

def layer_backward(grad_out, w_in, w_out, saved, need_input):
    inputs_f32, inv_rms, normed, pre_act, activated = saved
    in_scale = w_in.shape[1] ** (-0.5)
    out_scale = w_out.shape[0] ** (-0.5)
    grad_w_out = lax.dot_general(activated, grad_out, (((0,), (0,)), ((), ())), preferred_element_type=jnp.float32) * out_scale
    grad_act = lax.dot_general(grad_out, w_out, (((1,), (1,)), ((), ())), preferred_element_type=jnp.float32) * out_scale
    sigmoid_pre = jax.nn.sigmoid(pre_act)
    grad_pre = (grad_act * sigmoid_pre * (1.0 + pre_act * (1.0 - sigmoid_pre))).astype(jnp.bfloat16)
    grad_w_in = lax.dot_general(grad_pre, normed, (((0,), (0,)), ((), ())), preferred_element_type=jnp.float32) * in_scale
    if not need_input:
        return (grad_w_in, grad_w_out, grad_out)
    grad_norm = jnp.dot(grad_pre, w_in, preferred_element_type=jnp.float32) * in_scale
    inner_sum = lax.optimization_barrier(jnp.sum(grad_norm * inputs_f32, axis=-1, keepdims=True)) / inputs_f32.shape[1]
    grad_in = grad_out.astype(jnp.float32) + inv_rms * grad_norm - inputs_f32 * (inv_rms * inv_rms * inv_rms) * inner_sum
    return (grad_w_in, grad_w_out, grad_in.astype(jnp.bfloat16))

def reference(inputs, cotangent, weights, first_moment, second_moment, anchor, momentum, fragment):
    count = fragment[0].astype(jnp.int32)
    chosen = jnp.remainder(count, L).astype(jnp.int32)
    count_real = count.astype(jnp.float32)
    correct_one = 1.0 - jnp.exp(count_real * math.log(beta_one))
    correct_two = 1.0 - jnp.exp(count_real * math.log(beta_two))
    updated_all = []
    total = jnp.zeros(anchor.shape, jnp.float32)
    for replica in range(N_REP):
        params = weights[replica]
        packed = params.astype(jnp.bfloat16).reshape(L, 2, H, D)
        current = inputs[replica]
        saved_list = []
        for layer_index in range(L):
            current, saved = layer_forward(current, packed[layer_index, 0], packed[layer_index, 1])
            saved_list.append(saved)
        upstream = cotangent[replica]
        grads = [None] * L
        for layer_index in reversed(range(L)):
            grad_w_in, grad_w_out, upstream = layer_backward(upstream, packed[layer_index, 0], packed[layer_index, 1], saved_list[layer_index], layer_index > 0)
            grads[layer_index] = jnp.stack([grad_w_in, grad_w_out]).reshape(FLAT, 128)
        gradient = jnp.stack(grads) / (TOK_DEV * N_FSDP)
        moment_one = beta_one * first_moment[replica] + (1.0 - beta_one) * gradient
        moment_two = beta_two * second_moment[replica] + (1.0 - beta_two) * gradient * gradient
        updated = params - inner_rate * (moment_one / correct_one / (jnp.sqrt(moment_two / correct_two) + adam_eps) + decay_rate * params)
        updated_all.append(updated)
        total = total + (anchor - lax.dynamic_index_in_dim(params, chosen, 0, keepdims=False))
    mean_delta = total / N_REP
    new_momentum = outer_beta * momentum + mean_delta
    new_anchor = anchor - outer_rate * (mean_delta + outer_beta * new_momentum)
    selector = (jnp.arange(L, dtype=jnp.int32) == chosen)[:, None, None]
    merged = [jnp.where(selector, mixing * upd + (1.0 - mixing) * new_anchor[None], upd) for upd in updated_all]
    return (jnp.stack(merged), new_anchor, new_momentum)
```

```python
import math

import jax
import jax.numpy as jnp
from jax import lax
from jax.experimental import pallas as pl
from jax.experimental.pallas import tpu as pltpu
from jax.sharding import PartitionSpec as P

norm_eps = 1e-05
beta_one = 0.9
beta_two = 0.95
adam_eps = 1e-08
decay_rate = 0.1
inner_rate = 0.05
outer_rate = 0.7
outer_beta = 0.9
mixing = 0.5

MESH = pl.DeviceIdType.MESH
TOK = 128
D = 7168
H = 32
ROWS = 56
PLANE = 16
REPS = 8
F32 = jnp.float32
BF16 = jnp.bfloat16
CHIP = 2 * TOK
GRADS = CHIP
STACK = 2 * CHIP
ALL = STACK + 4 * H

NT = (((1,), (1,)), ((), ()))
NN = (((1,), (0,)), ((), ()))


def dot(a, b, dims):
    return lax.dot_general(a, b, dims, preferred_element_type=F32)


def kernel(
    x_h, g_h, w_h, fm_h, sm_h, an_h, mo_h, fr,
    new_w, new_a, new_m,
    stack, w_all, send, recv, z_send, z_recv, w_own, fm, sm, an, mo, rep_send, rep_recv,
    proj, coef, expand, flat, ss,
    load_sem, z_sems, ring_send, ring_recv, fwd_send, fwd_recv, tok_send, tok_recv,
    red_send, red_recv, rep_sems, rep_rsem,
):
    rep = lax.axis_index("rep")
    fsdp = lax.axis_index("fsdp")
    place = fsdp // 4
    zh = (fsdp // 2) % 2
    core = fsdp % 2

    def peer(k):
        return lax.rem(place + k, PLANE)

    def in_plane(q):
        return (rep, q * 4 + zh * 2 + core)

    other_z = (rep, place * 4 + (1 - zh) * 2 + core)
    sibling = (rep, place * 4 + zh * 2 + (1 - core))

    def rep_peer(k):
        return (lax.rem(rep + k, REPS), fsdp)

    def remote(src, dst, ssem, rsem, device):
        return pltpu.make_async_remote_copy(
            src_ref=src, dst_ref=dst, send_sem=ssem, recv_sem=rsem, device_id=device, device_id_type=MESH
        )

    barrier = pltpu.get_barrier_semaphore()

    def greet(device):
        pl.semaphore_signal(barrier, inc=1, device_id=device, device_id_type=MESH)

    greet(other_z)

    def greet_rep(k, _):
        greet(rep_peer(k))
        return 0

    lax.fori_loop(1, REPS, greet_rep, 0)
    greet(sibling)

    def greet_plane(k, _):
        greet(in_plane(peer(k)))
        return 0

    lax.fori_loop(1, PLANE, greet_plane, 0)

    loads = [
        pltpu.make_async_copy(src, dst, load_sem.at[i])
        for i, (src, dst) in enumerate(
            [
                (w_h.at[0], w_own),
                (x_h.at[0], stack.at[pl.ds(0, TOK)]),
                (g_h.at[0], stack.at[pl.ds(GRADS, TOK)]),
                (fm_h.at[0], fm),
                (sm_h.at[0], sm),
                (an_h, an),
                (mo_h, mo),
            ]
        )
    ]
    for load in loads:
        load.start()
    loads[0].wait()
    flat[pl.ds(0, ROWS, stride=2), :] = w_own[0]
    flat[pl.ds(1, ROWS, stride=2), :] = w_own[1]
    w_all[0, 0, place] = flat[...].astype(BF16).reshape(ROWS, 2, 128)
    step = fr[0]
    chosen = lax.rem(step, 2).astype(F32)
    rep_send[...] = w_own[0] * (1.0 - chosen) + w_own[1] * chosen

    pl.semaphore_wait(barrier, 1 + 1 + (PLANE - 1) + (REPS - 1))

    z_copy = remote(w_all.at[0, 0, place], w_all.at[1, 0, place], z_sems.at[0], z_sems.at[1], other_z)
    z_copy.start()

    def spread(h):
        def one(k, _):
            remote(
                w_all.at[h, 0, place], w_all.at[h, 0, place], ring_send.at[h], ring_recv.at[h, place], in_plane(peer(k))
            ).start()
            return 0

        lax.fori_loop(1, PLANE, one, 0)

    def hand_on(h, q):
        remote(w_all.at[h, 0, q], w_all.at[h, 1, q], fwd_send.at[h], fwd_recv.at[h], sibling).start()

    def collect(h):
        def one(k, _):
            q = lax.rem(place + PLANE - k, PLANE)
            remote(
                w_all.at[h, 0, q], w_all.at[h, 0, q], ring_send.at[h], ring_recv.at[h, q], in_plane(q)
            ).wait_recv()
            hand_on(h, q)
            return 0

        lax.fori_loop(1, PLANE, one, 0)

    spread(0)
    hand_on(0, place)
    tok_copies = []
    for i, start in enumerate((0, GRADS)):
        loads[1 + i].wait()
        copy = remote(
            stack.at[pl.ds(start, TOK)], stack.at[pl.ds(start + TOK, TOK)], tok_send.at[i], tok_recv.at[i], sibling
        )
        copy.start()
        tok_copies.append(copy)
    collect(0)
    z_copy.wait_recv()
    spread(1)
    hand_on(1, place)

    def rep_out(k, _):
        remote(rep_send, rep_recv.at[rep], rep_sems, rep_rsem.at[rep], rep_peer(k)).start()
        return 0

    lax.fori_loop(1, REPS, rep_out, 0)

    def relayout(h):
        remote(w_all.at[h, 0], w_all.at[h, 1], fwd_send.at[h], fwd_recv.at[h], sibling).wait_recv()

        def one(r, _):
            at = pl.multiple_of(r * 128, 128)
            for c in range(2):
                stack[pl.ds(STACK + h * 64 + c * 32, 32), pl.ds(at, 128)] = w_all[h, c, :, r].reshape(32, 128)
            return 0

        lax.fori_loop(0, ROWS, one, 0, unroll=4)

    relayout(0)
    for copy in tok_copies:
        copy.wait_recv()

    def square(r, acc):
        v = stack[pl.ds(0, CHIP), pl.ds(pl.multiple_of(r * 128, 128), 128)].astype(F32)
        return acc + v * v

    acc = lax.fori_loop(0, ROWS, square, jnp.zeros((CHIP, 128), F32))
    ss[...] = jnp.sum(acc.T, axis=0, keepdims=True)

    collect(1)
    relayout(1)

    proj[...] = jnp.zeros_like(proj)

    def project(i, _):
        at = pl.multiple_of(i * 1024, 1024)
        out = dot(stack[pl.ds(STACK, 4 * H), pl.ds(at, 1024)], stack[:, pl.ds(at, 1024)], NT)
        for j in range(ALL // 128):
            proj[j] += out[:, j * 128 : (j + 1) * 128]
        return 0

    lax.fori_loop(0, D // 1024, project, 0)

    def rows_of(kind, layer, cols):
        return jnp.concatenate(
            [
                jnp.concatenate([proj[j, pl.ds(hc * 32 + kind * 16 + layer, 8, stride=2), :] for hc in range(4)], axis=0)
                for j in cols
            ],
            axis=1,
        )

    tokens, grads, units = (0, 1), (2, 3), (4,)
    in_scale = D ** (-0.5)
    out_scale = H ** (-0.5)

    def put(kind, layer, v):
        expand[...] = jnp.zeros_like(expand)
        for j in range(2):
            for hc in range(4):
                expand[j, pl.ds(hc * 32 + kind * 16 + layer, 8, stride=2), :] = v[
                    hc * 8 : hc * 8 + 8, j * 128 : (j + 1) * 128
                ]
        return jnp.concatenate([expand[0], expand[1]], axis=1).astype(BF16)

    ss0 = ss[...]
    inv0 = lax.rsqrt(ss0 * (1.0 / D) + norm_eps)
    pre0 = rows_of(0, 0, tokens) * (inv0 * in_scale)
    sig0 = jax.nn.sigmoid(pre0)
    act0 = pre0 * sig0 * out_scale
    out0_h = rows_of(1, 0, tokens)
    gram = jnp.concatenate([rows_of(0, 1, units), rows_of(1, 0, units)], axis=0).astype(BF16)
    act_e = put(1, 0, act0)
    mixed = dot(gram, act_e, NN)
    in1_h1 = rows_of(0, 1, tokens) + mixed[0:H]
    out0_h1 = out0_h + mixed[H : 2 * H]
    ss1 = ss0 + jnp.sum(act0 * (out0_h + out0_h1), axis=0, keepdims=True)
    inv1 = lax.rsqrt(jnp.maximum(ss1, 0.0) * (1.0 / D) + norm_eps)
    pre1 = in1_h1 * (inv1 * in_scale)
    sig1 = jax.nn.sigmoid(pre1)
    act1 = pre1 * sig1 * out_scale
    grad_pre1 = rows_of(1, 1, grads) * out_scale * sig1 * (1.0 + pre1 * (1.0 - sig1))
    back = grad_pre1 * (inv1 * in_scale)
    pull = (inv1 * inv1 * (1.0 / D)) * jnp.sum(back * in1_h1, axis=0, keepdims=True)
    back_e = put(0, 1, back)
    grad_act0 = rows_of(1, 0, grads) + dot(gram[H : 2 * H], back_e, NN) - pull * out0_h1
    grad_pre0 = grad_act0 * out_scale * sig0 * (1.0 + pre0 * (1.0 - sig0))

    act0_b = act0.astype(BF16)
    pulled = act0 * pull
    mix1 = dot(back.astype(BF16), act_e, NT)
    mix0 = dot(act0_b, back_e, NT) - dot(pulled.astype(BF16), act_e, NT)
    zero = jnp.zeros((H, CHIP), F32)
    zero_u = jnp.zeros((H, 4 * H), F32)
    for kind, layer, parts in (
        (0, 0, (grad_pre0 * (inv0 * in_scale), zero, zero_u)),
        (0, 1, (back, zero, mix1)),
        (1, 0, (-pulled, act0, mix0)),
        (1, 1, (zero, act1, zero_u)),
    ):
        for h in range(2):
            for part, cols in zip(parts, (tokens, grads, units), strict=True):
                for i, j in enumerate(cols):
                    coef[j, pl.ds(h * 32 + kind * 16 + layer, 8, stride=2), :] = part[
                        h * 16 : h * 16 + 8, i * 128 : (i + 1) * 128
                    ]

    def gradients(h):
        weights = jnp.concatenate([coef[j, pl.ds(h * 32, 32), :] for j in range(ALL // 128)], axis=1).astype(BF16)

        def one(i, _):
            at = pl.multiple_of(i * 512, 512)
            out = dot(weights, stack[:, pl.ds(at, 512)], NN).astype(BF16)
            for j in range(4):
                send[h, :, i * 4 + j] = out[:, j * 128 : (j + 1) * 128].reshape(PLANE, 2, 128)
            return 0

        lax.fori_loop(0, D // 512, one, 0)

        def out_one(k, _):
            q = peer(k)
            remote(
                send.at[h, q], recv.at[h, place], red_send.at[h], red_recv.at[h], in_plane(q)
            ).start()
            return 0

        lax.fori_loop(1, PLANE, out_one, 0)
        recv[h, place] = send[h, place]

    def summed(h):
        pltpu.make_async_copy(
            recv.at[h, pl.ds(0, PLANE - 1)], recv.at[h, pl.ds(0, PLANE - 1)], red_recv.at[h]
        ).wait()
        total = recv[h, 0].reshape(2 * ROWS, 128).astype(F32)
        for q in range(1, PLANE):
            total += recv[h, q].reshape(2 * ROWS, 128).astype(F32)
        return total

    gradients(1)
    gradients(0)
    z_send[...] = summed(1).astype(BF16).reshape(ROWS, 2, 128)
    z_back = remote(z_send, z_recv, z_sems.at[2], z_sems.at[3], other_z)
    z_back.start()

    for load in loads[3:]:
        load.wait()

    def rep_in(k, _):
        q = lax.rem(rep + k, REPS)
        remote(rep_send, rep_recv.at[q], rep_sems, rep_rsem.at[q], rep_peer(k)).wait_recv()
        return 0

    lax.fori_loop(1, REPS, rep_in, 0)
    rep_recv[rep] = rep_send[...]
    anchor = an[...]
    total = anchor - rep_recv[0]
    for q in range(1, REPS):
        total += anchor - rep_recv[q]
    delta = total * (1.0 / REPS)
    velocity = outer_beta * mo[...] + delta
    new_anchor = anchor - outer_rate * (delta + outer_beta * velocity)
    new_m[...] = velocity
    new_a[...] = new_anchor

    own = summed(0)
    z_back.wait_recv()
    flat[...] = (own + z_recv[...].reshape(2 * ROWS, 128).astype(F32)) * (1.0 / (TOK * 64))
    count = jnp.full((8, 128), step.astype(F32), F32)
    correct_one = (1.0 - jnp.exp(count * math.log(beta_one)))[0:1]
    correct_two = (1.0 - jnp.exp(count * math.log(beta_two)))[0:1]
    for layer in range(2):
        gradient = flat[pl.ds(layer, ROWS, stride=2), :]
        params = w_own[layer]
        one = beta_one * fm[layer] + (1.0 - beta_one) * gradient
        two = beta_two * sm[layer] + (1.0 - beta_two) * gradient * gradient
        updated = params - inner_rate * (
            one / correct_one / (jnp.sqrt(two / correct_two) + adam_eps) + decay_rate * params
        )
        merged = mixing * updated + (1.0 - mixing) * new_anchor
        here = chosen if layer == 1 else 1.0 - chosen
        new_w[0, layer] = jnp.where(jnp.full((ROWS, 128), here, F32) > 0.5, merged, updated)

    z_copy.wait_send()
    z_back.wait_send()
    for copy in tok_copies:
        copy.wait_send()
    for h in range(2):
        most = w_all.at[h, 0, pl.ds(0, PLANE - 1)]
        pltpu.make_async_copy(most, most, ring_send.at[h]).wait()
        pltpu.make_async_copy(w_all.at[h, 0], w_all.at[h, 0], fwd_send.at[h]).wait()
        most = send.at[h, pl.ds(0, PLANE - 1)]
        pltpu.make_async_copy(most, most, red_send.at[h]).wait()
    most = rep_recv.at[pl.ds(0, REPS - 1)]
    pltpu.make_async_copy(most, most, rep_sems).wait()


def shards(inputs, cotangent, weights, first_moment, second_moment, anchor, momentum, fragment):
    any_space = pl.BlockSpec(memory_space=pl.ANY)
    vmem = pl.BlockSpec(memory_space=pltpu.VMEM)
    dma = pltpu.SemaphoreType.DMA
    unit = (ROWS, 2, 128)
    return pl.pallas_call(
        kernel,
        out_shape=(
            jax.ShapeDtypeStruct((1, 2, ROWS, 128), F32),
            jax.ShapeDtypeStruct((ROWS, 128), F32),
            jax.ShapeDtypeStruct((ROWS, 128), F32),
        ),
        in_specs=[any_space] * 7 + [pl.BlockSpec(memory_space=pltpu.SMEM)],
        out_specs=(vmem, vmem, vmem),
        scratch_shapes=[
            pltpu.VMEM((ALL, D), BF16),
            pltpu.VMEM((2, 2, PLANE) + unit, BF16),
            pltpu.VMEM((2, PLANE) + unit, BF16),
            pltpu.VMEM((2, PLANE) + unit, BF16),
            pltpu.VMEM(unit, BF16),
            pltpu.VMEM(unit, BF16),
            pltpu.VMEM((2, ROWS, 128), F32),
            pltpu.VMEM((2, ROWS, 128), F32),
            pltpu.VMEM((2, ROWS, 128), F32),
            pltpu.VMEM((ROWS, 128), F32),
            pltpu.VMEM((ROWS, 128), F32),
            pltpu.VMEM((ROWS, 128), F32),
            pltpu.VMEM((REPS, ROWS, 128), F32),
            pltpu.VMEM((ALL // 128, 4 * H, 128), F32),
            pltpu.VMEM((ALL // 128, 2 * H, 128), F32),
            pltpu.VMEM((2, 4 * H, 128), F32),
            pltpu.VMEM((2 * ROWS, 128), F32),
            pltpu.VMEM((1, CHIP), F32),
            dma((7,)),
            dma((4,)),
            dma((2,)),
            dma((2, PLANE)),
            dma((2,)),
            dma((2,)),
            dma((2,)),
            dma((2,)),
            dma((2,)),
            dma((2,)),
            dma,
            dma((REPS,)),
        ],
        compiler_params=pltpu.CompilerParams(
            collective_id=0, has_side_effects=True, vmem_limit_bytes=56 * 1024 * 1024
        ),
        name="window",
    )(inputs, cotangent, weights, first_moment, second_moment, anchor, momentum, fragment)


def solution(mesh):
    placed = (
        P("rep", "fsdp", None),
        P("rep", "fsdp", None),
        P("rep", None, "fsdp", None),
        P("rep", None, "fsdp", None),
        P("rep", None, "fsdp", None),
        P("fsdp", None),
        P("fsdp", None),
        P(),
    )
    return jax.shard_map(
        shards,
        mesh=mesh,
        in_specs=placed,
        out_specs=(P("rep", None, "fsdp", None), P("fsdp", None), P("fsdp", None)),
        check_vma=False,
    )
```

```python
import math

import jax
import jax.numpy as jnp
from jax import lax
from jax.experimental import pallas as pl
from jax.experimental.pallas import tpu as pltpu
from jax.sharding import PartitionSpec as P

norm_eps = 1e-05
beta_one = 0.9
beta_two = 0.95
adam_eps = 1e-08
decay_rate = 0.1
inner_rate = 0.05
outer_rate = 0.7
outer_beta = 0.9
mixing = 0.5

MESH = pl.DeviceIdType.MESH
TOK = 128
D = 7168
H = 32
ROWS = 56
PLANE = 16
REPS = 8
F32 = jnp.float32
BF16 = jnp.bfloat16
CHIP = 2 * TOK
GRADS = CHIP
STACK = 2 * CHIP
ALL = STACK + 4 * H

NT = (((1,), (1,)), ((), ()))
NN = (((1,), (0,)), ((), ()))


def dot(a, b, dims):
    return lax.dot_general(a, b, dims, preferred_element_type=F32)


def kernel(
    x_h, g_h, w_h, fm_h, sm_h, an_h, mo_h, fr_h,
    new_w, new_a, new_m,
    stack, across, w_all, send, recv, z_send, z_recv, w_own, fm, sm, an, mo, rep_send, rep_recv,
    proj, coef, expand, flat, ss,
    step_s, load_sem, z_sems, ring_send, ring_recv, fwd_send, fwd_recv, tok_send, tok_recv,
    red_send, red_recv, rep_sems, rep_rsem,
):
    rep = lax.axis_index("rep")
    fsdp = lax.axis_index("fsdp")
    place = fsdp // 4
    zh = (fsdp // 2) % 2
    core = fsdp % 2

    def peer(k):
        return lax.rem(place + k, PLANE)

    def in_plane(q):
        return (rep, q * 4 + zh * 2 + core)

    other_z = (rep, place * 4 + (1 - zh) * 2 + core)
    sibling = (rep, place * 4 + zh * 2 + (1 - core))

    def rep_peer(k):
        return (lax.rem(rep + k, REPS), fsdp)

    def remote(src, dst, ssem, rsem, device):
        return pltpu.make_async_remote_copy(
            src_ref=src, dst_ref=dst, send_sem=ssem, recv_sem=rsem, device_id=device, device_id_type=MESH
        )

    barrier = pltpu.get_barrier_semaphore()

    def greet(device):
        pl.semaphore_signal(barrier, inc=1, device_id=device, device_id_type=MESH)

    greet(other_z)

    def greet_rep(k, _):
        greet(rep_peer(k))
        return 0

    lax.fori_loop(1, REPS, greet_rep, 0)
    greet(sibling)

    def greet_plane(k, _):
        greet(in_plane(peer(k)))
        return 0

    lax.fori_loop(1, PLANE, greet_plane, 0)

    loads = [
        pltpu.make_async_copy(src, dst, load_sem.at[i])
        for i, (src, dst) in enumerate(
            [
                (w_h.at[0], w_own),
                (x_h.at[0], stack.at[pl.ds(0, TOK)]),
                (g_h.at[0], stack.at[pl.ds(GRADS, TOK)]),
                (fm_h.at[0], fm),
                (sm_h.at[0], sm),
                (an_h, an),
                (mo_h, mo),
                (fr_h, step_s),
            ]
        )
    ]
    for load in loads:
        load.start()
    loads[0].wait()
    flat[pl.ds(0, ROWS, stride=2), :] = w_own[0]
    flat[pl.ds(1, ROWS, stride=2), :] = w_own[1]
    w_all[0, 0, place] = flat[...].astype(BF16).reshape(ROWS, 2, 128)
    loads[7].wait()
    step = step_s[0]
    chosen = lax.rem(step, 2).astype(F32)
    rep_send[...] = w_own[0] * (1.0 - chosen) + w_own[1] * chosen

    def turn(start):
        def one(r, _):
            at = pl.multiple_of(r * 128, 128)
            across[pl.ds(at, 128), start : start + TOK] = stack[pl.ds(start, TOK), pl.ds(at, 128)].T
            return 0

        lax.fori_loop(0, ROWS, one, 0, unroll=14)

    loads[1].wait()
    turn(0)
    loads[2].wait()
    turn(GRADS)

    pl.semaphore_wait(barrier, 1 + 1 + (PLANE - 1) + (REPS - 1))

    z_copy = remote(w_all.at[0, 0, place], w_all.at[1, 0, place], z_sems.at[0], z_sems.at[1], other_z)
    z_copy.start()

    def spread(h):
        def one(k, _):
            remote(
                w_all.at[h, 0, place], w_all.at[h, 0, place], ring_send.at[h], ring_recv.at[h, place], in_plane(peer(k))
            ).start()
            return 0

        lax.fori_loop(1, PLANE, one, 0)

    def hand_on(h, q):
        remote(w_all.at[h, 0, q], w_all.at[h, 1, q], fwd_send.at[h], fwd_recv.at[h], sibling).start()

    def collect(h):
        def one(k, _):
            q = lax.rem(place + PLANE - k, PLANE)
            remote(
                w_all.at[h, 0, q], w_all.at[h, 0, q], ring_send.at[h], ring_recv.at[h, q], in_plane(q)
            ).wait_recv()
            hand_on(h, q)
            return 0

        lax.fori_loop(1, PLANE, one, 0)

    spread(0)
    hand_on(0, place)
    tok_copies = []
    for i, start in enumerate((0, GRADS)):
        copy = remote(
            stack.at[pl.ds(start, TOK)], stack.at[pl.ds(start + TOK, TOK)], tok_send.at[i], tok_recv.at[i], sibling
        )
        copy.start()
        tok_copies.append(copy)

    def relayout(h):
        remote(w_all.at[h, 0], w_all.at[h, 1], fwd_send.at[h], fwd_recv.at[h], sibling).wait_recv()

        def one(r, _):
            at = pl.multiple_of(r * 128, 128)
            for c in range(2):
                stack[pl.ds(STACK + h * 64 + c * 32, 32), pl.ds(at, 128)] = w_all[h, c, :, r].reshape(32, 128)
            return 0

        lax.fori_loop(0, ROWS, one, 0, unroll=8)

    collect(0)
    relayout(0)
    z_copy.wait_recv()
    spread(1)
    hand_on(1, place)

    def rep_out(k, _):
        remote(rep_send, rep_recv.at[rep], rep_sems, rep_rsem.at[rep], rep_peer(k)).start()
        return 0

    lax.fori_loop(1, REPS, rep_out, 0)

    for copy, start in zip(tok_copies, (TOK, GRADS + TOK), strict=True):
        copy.wait_recv()
        turn(start)

    def square(r, acc):
        v = across[pl.ds(pl.multiple_of(r * 128, 128), 128), 0:CHIP].astype(F32)
        v = v * v
        for i in range(16):
            acc += v[i * 8 : i * 8 + 8]
        return acc

    acc = lax.fori_loop(0, ROWS, square, jnp.zeros((8, CHIP), F32), unroll=4)
    ss[...] = jnp.sum(acc, axis=0, keepdims=True)

    collect(1)
    relayout(1)

    with_tokens = dot(stack[STACK:ALL, :], across[...], NN)
    for j in range(STACK // 128):
        proj[j] = with_tokens[:, j * 128 : (j + 1) * 128]
    proj[STACK // 128] = dot(stack[STACK:ALL, :], stack[STACK:ALL, :], NT)

    def rows_of(kind, layer, cols):
        return jnp.concatenate(
            [
                jnp.concatenate([proj[j, pl.ds(hc * 32 + kind * 16 + layer, 8, stride=2), :] for hc in range(4)], axis=0)
                for j in cols
            ],
            axis=1,
        )

    tokens, grads, units = (0, 1), (2, 3), (4,)
    in_scale = D ** (-0.5)
    out_scale = H ** (-0.5)

    def put(kind, layer, v):
        expand[...] = jnp.zeros_like(expand)
        for j in range(2):
            for hc in range(4):
                expand[j, pl.ds(hc * 32 + kind * 16 + layer, 8, stride=2), :] = v[
                    hc * 8 : hc * 8 + 8, j * 128 : (j + 1) * 128
                ]
        return jnp.concatenate([expand[0], expand[1]], axis=1).astype(BF16)

    ss0 = ss[...]
    inv0 = lax.rsqrt(ss0 * (1.0 / D) + norm_eps)
    pre0 = rows_of(0, 0, tokens) * (inv0 * in_scale)
    sig0 = jax.nn.sigmoid(pre0)
    act0 = pre0 * sig0 * out_scale
    out0_h = rows_of(1, 0, tokens)
    gram = jnp.concatenate([rows_of(0, 1, units), rows_of(1, 0, units)], axis=0).astype(BF16)
    act_e = put(1, 0, act0)
    mixed = dot(gram, act_e, NN)
    in1_h1 = rows_of(0, 1, tokens) + mixed[0:H]
    out0_h1 = out0_h + mixed[H : 2 * H]
    ss1 = ss0 + jnp.sum(act0 * (out0_h + out0_h1), axis=0, keepdims=True)
    inv1 = lax.rsqrt(jnp.maximum(ss1, 0.0) * (1.0 / D) + norm_eps)
    pre1 = in1_h1 * (inv1 * in_scale)
    sig1 = jax.nn.sigmoid(pre1)
    act1 = pre1 * sig1 * out_scale
    grad_pre1 = rows_of(1, 1, grads) * out_scale * sig1 * (1.0 + pre1 * (1.0 - sig1))
    back = grad_pre1 * (inv1 * in_scale)
    pull = (inv1 * inv1 * (1.0 / D)) * jnp.sum(back * in1_h1, axis=0, keepdims=True)
    back_e = put(0, 1, back)
    grad_act0 = rows_of(1, 0, grads) + dot(gram[H : 2 * H], back_e, NN) - pull * out0_h1
    grad_pre0 = grad_act0 * out_scale * sig0 * (1.0 + pre0 * (1.0 - sig0))

    act0_b = act0.astype(BF16)
    pulled = act0 * pull
    mix1 = dot(back.astype(BF16), act_e, NT)
    mix0 = dot(act0_b, back_e, NT) - dot(pulled.astype(BF16), act_e, NT)
    zero = jnp.zeros((H, CHIP), F32)
    zero_u = jnp.zeros((H, 4 * H), F32)
    for kind, layer, parts in (
        (0, 0, (grad_pre0 * (inv0 * in_scale), zero, zero_u)),
        (0, 1, (back, zero, mix1)),
        (1, 0, (-pulled, act0, mix0)),
        (1, 1, (zero, act1, zero_u)),
    ):
        for h in range(2):
            for part, cols in zip(parts, (tokens, grads, units), strict=True):
                for i, j in enumerate(cols):
                    coef[j, pl.ds(h * 32 + kind * 16 + layer, 8, stride=2), :] = part[
                        h * 16 : h * 16 + 8, i * 128 : (i + 1) * 128
                    ]

    def gradients(h):
        weights = jnp.concatenate(
            [coef[j, pl.ds(pl.multiple_of(h * 32, 32), 32), :] for j in range(ALL // 128)], axis=1
        ).astype(BF16)
        for part in range(2):
            first = part * (ROWS // 2)
            out = dot(weights, stack[:, first * 128 : (first + ROWS // 2) * 128], NN).astype(BF16)
            for j in range(ROWS // 2):
                send[h, :, first + j] = out[:, j * 128 : (j + 1) * 128].reshape(PLANE, 2, 128)
            rows = pl.ds(first, ROWS // 2)

            def out_one(k, _, rows=rows):
                q = peer(k)
                remote(
                    send.at[h, q, rows], recv.at[h, place, rows], red_send.at[h], red_recv.at[h], in_plane(q)
                ).start()
                return 0

            lax.fori_loop(1, PLANE, out_one, 0)
        recv[h, place] = send[h, place]

    def summed(h):
        pltpu.make_async_copy(
            recv.at[h, pl.ds(0, PLANE - 1)], recv.at[h, pl.ds(0, PLANE - 1)], red_recv.at[h]
        ).wait()
        total = recv[h, 0].reshape(2 * ROWS, 128).astype(F32)
        for q in range(1, PLANE):
            total += recv[h, q].reshape(2 * ROWS, 128).astype(F32)
        return total

    gradients(zh)
    gradients(1 - zh)
    z_send[...] = summed(1).astype(BF16).reshape(ROWS, 2, 128)
    z_back = remote(z_send, z_recv, z_sems.at[2], z_sems.at[3], other_z)
    z_back.start()

    for load in loads[3:7]:
        load.wait()

    def rep_in(k, _):
        q = lax.rem(rep + k, REPS)
        remote(rep_send, rep_recv.at[q], rep_sems, rep_rsem.at[q], rep_peer(k)).wait_recv()
        return 0

    lax.fori_loop(1, REPS, rep_in, 0)
    rep_recv[rep] = rep_send[...]
    anchor = an[...]
    total = anchor - rep_recv[0]
    for q in range(1, REPS):
        total += anchor - rep_recv[q]
    delta = total * (1.0 / REPS)
    velocity = outer_beta * mo[...] + delta
    new_anchor = anchor - outer_rate * (delta + outer_beta * velocity)
    new_m[...] = velocity
    new_a[...] = new_anchor

    own = summed(0)
    z_back.wait_recv()
    flat[...] = (own + z_recv[...].reshape(2 * ROWS, 128).astype(F32)) * (1.0 / (TOK * 64))
    count = jnp.full((8, 128), step.astype(F32), F32)
    correct_one = (1.0 - jnp.exp(count * math.log(beta_one)))[0:1]
    correct_two = (1.0 - jnp.exp(count * math.log(beta_two)))[0:1]
    for layer in range(2):
        gradient = flat[pl.ds(layer, ROWS, stride=2), :]
        params = w_own[layer]
        one = beta_one * fm[layer] + (1.0 - beta_one) * gradient
        two = beta_two * sm[layer] + (1.0 - beta_two) * gradient * gradient
        updated = params - inner_rate * (
            one / correct_one / (jnp.sqrt(two / correct_two) + adam_eps) + decay_rate * params
        )
        merged = mixing * updated + (1.0 - mixing) * new_anchor
        here = chosen if layer == 1 else 1.0 - chosen
        new_w[0, layer] = jnp.where(jnp.full((ROWS, 128), here, F32) > 0.5, merged, updated)

    z_copy.wait_send()
    z_back.wait_send()
    for copy in tok_copies:
        copy.wait_send()
    for h in range(2):
        most = w_all.at[h, 0, pl.ds(0, PLANE - 1)]
        pltpu.make_async_copy(most, most, ring_send.at[h]).wait()
        pltpu.make_async_copy(w_all.at[h, 0], w_all.at[h, 0], fwd_send.at[h]).wait()
        most = send.at[h, pl.ds(0, PLANE - 1)]
        pltpu.make_async_copy(most, most, red_send.at[h]).wait()
    most = rep_recv.at[pl.ds(0, REPS - 1)]
    pltpu.make_async_copy(most, most, rep_sems).wait()


def place_results(a, b, c, to_a, to_b, to_c):
    to_a[...] = a[...]
    to_b[...] = b[...]
    to_c[...] = c[...]


def shards(inputs, cotangent, weights, first_moment, second_moment, anchor, momentum, fragment):
    hbm = pl.BlockSpec(memory_space=pltpu.HBM)
    vmem = pl.BlockSpec(memory_space=pltpu.VMEM)
    dma = pltpu.SemaphoreType.DMA
    unit = (ROWS, 2, 128)
    results = pl.pallas_call(
        kernel,
        out_shape=(
            pltpu.VMEM((1, 2, ROWS, 128), F32),
            pltpu.VMEM((ROWS, 128), F32),
            pltpu.VMEM((ROWS, 128), F32),
        ),
        in_specs=[hbm] * 8,
        out_specs=(vmem, vmem, vmem),
        scratch_shapes=[
            pltpu.VMEM((ALL, D), BF16),
            pltpu.VMEM((D, STACK), BF16),
            pltpu.VMEM((2, 2, PLANE) + unit, BF16),
            pltpu.VMEM((2, PLANE) + unit, BF16),
            pltpu.VMEM((2, PLANE) + unit, BF16),
            pltpu.VMEM(unit, BF16),
            pltpu.VMEM(unit, BF16),
            pltpu.VMEM((2, ROWS, 128), F32),
            pltpu.VMEM((2, ROWS, 128), F32),
            pltpu.VMEM((2, ROWS, 128), F32),
            pltpu.VMEM((ROWS, 128), F32),
            pltpu.VMEM((ROWS, 128), F32),
            pltpu.VMEM((ROWS, 128), F32),
            pltpu.VMEM((REPS, ROWS, 128), F32),
            pltpu.VMEM((ALL // 128, 4 * H, 128), F32),
            pltpu.VMEM((ALL // 128, 2 * H, 128), F32),
            pltpu.VMEM((2, 4 * H, 128), F32),
            pltpu.VMEM((2 * ROWS, 128), F32),
            pltpu.VMEM((1, CHIP), F32),
            pltpu.SMEM((1,), jnp.int32),
            dma((8,)),
            dma((4,)),
            dma((2,)),
            dma((2, PLANE)),
            dma((2,)),
            dma((2,)),
            dma((2,)),
            dma((2,)),
            dma((2,)),
            dma((2,)),
            dma,
            dma((REPS,)),
        ],
        compiler_params=pltpu.CompilerParams(
            collective_id=0, has_side_effects=True, vmem_limit_bytes=56 * 1024 * 1024
        ),
        name="window",
    )(
        *(
            a
            for a in (inputs, cotangent, weights, first_moment, second_moment, anchor, momentum, fragment)
        )
    )
    return pl.pallas_call(
        place_results,
        out_shape=tuple(jax.ShapeDtypeStruct(r.shape, r.dtype) for r in results),
        in_specs=[vmem] * 3,
        out_specs=(vmem,) * 3,
        name="results",
    )(*(pltpu.with_memory_space_constraint(r, pltpu.VMEM) for r in results))


def solution(mesh):
    placed = (
        P("rep", "fsdp", None),
        P("rep", "fsdp", None),
        P("rep", None, "fsdp", None),
        P("rep", None, "fsdp", None),
        P("rep", None, "fsdp", None),
        P("fsdp", None),
        P("fsdp", None),
        P(),
    )
    return jax.shard_map(
        shards,
        mesh=mesh,
        in_specs=placed,
        out_specs=(P("rep", None, "fsdp", None), P("fsdp", None), P("fsdp", None)),
        check_vma=False,
    )
```

```python
import math

import jax
import jax.numpy as jnp
from jax import lax
from jax.experimental import pallas as pl
from jax.experimental.pallas import tpu as pltpu
from jax.sharding import PartitionSpec as P

norm_eps = 1e-05
beta_one = 0.9
beta_two = 0.95
adam_eps = 1e-08
decay_rate = 0.1
inner_rate = 0.05
outer_rate = 0.7
outer_beta = 0.9
mixing = 0.5

MESH = pl.DeviceIdType.MESH
TOK = 128
D = 7168
H = 32
ROWS = 56
PLANE = 16
REPS = 8
F32 = jnp.float32
BF16 = jnp.bfloat16
CHIP = 2 * TOK
GRADS = CHIP
STACK = 2 * CHIP
ALL = STACK + 4 * H

NT = (((1,), (1,)), ((), ()))
NN = (((1,), (0,)), ((), ()))


def dot(a, b, dims):
    return lax.dot_general(a, b, dims, preferred_element_type=F32)


def kernel(
    x_h, g_h, w_h, fm_h, sm_h, an_h, mo_h, fr_h,
    new_w, new_a, new_m,
    stack, across, w_all, send, recv, z_send, z_recv, staged, w_own, fm, sm, an, mo, rep_send, rep_recv,
    proj, coef, expand, flat, ss,
    step_s, load_sem, z_out, z_in, z_back_sems, ring_send, ring_recv, fwd_send, fwd_recv, tok_send, tok_recv,
    red_send, red_recv, rep_out, rep_in, stage_out, stage_in, rest_out, there, ready,
):
    rep = lax.axis_index("rep")
    fsdp = lax.axis_index("fsdp")
    place = fsdp // 4
    zh = (fsdp // 2) % 2
    core = fsdp % 2

    def peer(k):
        return lax.rem(place + k, PLANE)

    def in_plane(q):
        return (rep, q * 4 + zh * 2 + core)

    early = zh == 0
    late = zh == 1
    other_z = (rep, place * 4 + (1 - zh) * 2 + core)
    sibling = (rep, place * 4 + zh * 2 + (1 - core))
    across_rep = (
        lax.rem(rep + 4, REPS),
        rep + 2 - 4 * lax.rem(rep // 2, 2),
        rep + 1 - 2 * lax.rem(rep, 2),
    )

    def remote(src, dst, ssem, rsem, device):
        return pltpu.make_async_remote_copy(
            src_ref=src, dst_ref=dst, send_sem=ssem, recv_sem=rsem, device_id=device, device_id_type=MESH
        )

    barrier = pltpu.get_barrier_semaphore()

    def greet(device):
        pl.semaphore_signal(barrier, inc=1, device_id=device, device_id_type=MESH)

    @pl.when(early & (core == 0))
    def _():
        greet((across_rep[0], fsdp))
        greet((rep, fsdp + 2))
        greet((across_rep[0], fsdp + 2))

    @pl.when(early & (core == 1))
    def _():
        greet((rep, fsdp + 2))

    @pl.when(late & (core == 1))
    def _():
        greet(sibling)

    for r in across_rep:
        greet((r, place * 4 + zh * 2 + 1))

    @pl.when(core == 0)
    def _():
        greet(sibling)

    def greet_plane(k, _):
        greet((rep, peer(k) * 4 + zh * 2 + 1))
        return 0

    lax.fori_loop(1, PLANE, greet_plane, 0)

    loads = [
        pltpu.make_async_copy(src, dst, load_sem.at[i])
        for i, (src, dst) in enumerate(
            [
                (w_h.at[0], w_own),
                (x_h.at[0], stack.at[pl.ds(0, TOK)]),
                (g_h.at[0], stack.at[pl.ds(GRADS, TOK)]),
                (fm_h.at[0], fm),
                (sm_h.at[0], sm),
                (an_h, an),
                (mo_h, mo),
                (fr_h, step_s),
            ]
        )
    ]
    for load in loads:
        load.start()
    loads[0].wait()
    flat[pl.ds(0, ROWS, stride=2), :] = w_own[0]
    flat[pl.ds(1, ROWS, stride=2), :] = w_own[1]
    w_all[0, 0, place] = flat[...].astype(BF16).reshape(ROWS, 2, 128)
    z_copy = remote(w_all.at[0, 0, place], w_all.at[1, 0, place], z_out.at[0], z_in.at[0], other_z)

    @pl.when(late & (core == 0))
    def _():
        pl.semaphore_wait(barrier, 3)
        pl.semaphore_signal(there, inc=1, device_id=(across_rep[0], fsdp - 2), device_id_type=MESH)
        z_copy.start()

    loads[7].wait()
    step = step_s[0]
    chosen = lax.rem(step, 2).astype(F32)
    loads[5].wait()
    rep_send[0] = an[...] - (w_own[0] * (1.0 - chosen) + w_own[1] * chosen)

    def turn(start):
        def one(r, _):
            at = pl.multiple_of(r * 128, 128)
            across[pl.ds(at, 128), start : start + TOK] = stack[pl.ds(start, TOK), pl.ds(at, 128)].T
            return 0

        lax.fori_loop(0, ROWS, one, 0, unroll=14)

    loads[1].wait()
    turn(0)
    loads[2].wait()
    turn(GRADS)

    @pl.when(core == 1)
    def _():
        pl.semaphore_wait(barrier, 2 * PLANE - 1 + 2 * len(across_rep) + zh)
        pl.semaphore_signal(ready, inc=1, device_id=sibling, device_id_type=MESH)

    @pl.when(core == 0)
    def _():
        pl.semaphore_wait(ready, 1)

    pair = remote(w_all.at[0, 0, place], w_all.at[0, 1, place], z_out.at[1], z_in.at[1], sibling)
    pair.start()

    @pl.when(late & (core == 1))
    def _():
        z_copy.start()

    def spread(h):
        def one(k, _):
            remote(
                w_all.at[h, 0, place], w_all.at[h, 0, place], ring_send.at[h], ring_recv.at[h, place], in_plane(peer(k))
            ).start()
            return 0

        lax.fori_loop(1, PLANE, one, 0)

    def hand_on(h, q):
        remote(w_all.at[h, 0, q], w_all.at[h, 1, q], fwd_send.at[h], fwd_recv.at[h], sibling).start()

    def collect(h):
        def one(k, _):
            q = lax.rem(place + PLANE - k, PLANE)
            remote(
                w_all.at[h, 0, q], w_all.at[h, 0, q], ring_send.at[h], ring_recv.at[h, q], in_plane(q)
            ).wait_recv()
            hand_on(h, q)
            return 0

        lax.fori_loop(1, PLANE, one, 0)

    spread(0)
    tok_copies = []
    for i, start in enumerate((0, GRADS)):
        copy = remote(
            stack.at[pl.ds(start, TOK)], stack.at[pl.ds(start + TOK, TOK)], tok_send.at[i], tok_recv.at[i], sibling
        )
        copy.start()
        tok_copies.append(copy)

    adds = [
        remote(rep_send.at[i], rep_recv.at[i], rep_out.at[i], rep_in.at[i], (across_rep[i], fsdp)) for i in range(3)
    ]
    adds[0].start()

    def hops():
        half = [
            remote(w_all.at[0, c, place], staged.at[c], stage_out.at[c], stage_in.at[c], (across_rep[0], fsdp))
            for c in range(2)
        ]
        rest = [
            remote(staged.at[c], w_all.at[1, 0, place], rest_out.at[c], z_in.at[0], (across_rep[0], fsdp + 2 + c))
            for c in range(2)
        ]
        return half, rest

    @pl.when(early & (core == 0))
    def _():
        half, rest = hops()
        pl.semaphore_wait(barrier, 1)
        pair.wait_recv()
        for copy in half:
            copy.start()
        for copy in half:
            copy.wait()
        pl.semaphore_wait(there, 1)
        for copy in rest:
            copy.start()

    @pl.when(late | (core == 1))
    def _():
        pair.wait_recv()

    z_copy.wait_recv()
    spread(1)
    hand_on(1, place)

    adds[0].wait_recv()
    rep_send[1] = rep_send[0] + rep_recv[0]
    adds[1].start()

    def relayout(h):
        most = w_all.at[h, 1, pl.ds(0, PLANE - 1 + h)]
        remote(most, most, fwd_send.at[h], fwd_recv.at[h], sibling).wait_recv()

        def one(r, _):
            at = pl.multiple_of(r * 128, 128)
            for c in range(2):
                stack[pl.ds(STACK + h * 64 + c * 32, 32), pl.ds(at, 128)] = w_all[h, c, :, r].reshape(32, 128)
            return 0

        lax.fori_loop(0, ROWS, one, 0, unroll=8)

    for copy, start in zip(tok_copies, (TOK, GRADS + TOK), strict=True):
        copy.wait_recv()
        turn(start)

    def square(r, acc):
        v = across[pl.ds(pl.multiple_of(r * 128, 128), 128), 0:CHIP].astype(F32)
        v = v * v
        for i in range(16):
            acc += v[i * 8 : i * 8 + 8]
        return acc

    acc = lax.fori_loop(0, ROWS, square, jnp.zeros((8, CHIP), F32), unroll=4)
    ss[...] = jnp.sum(acc, axis=0, keepdims=True)

    collect(0)
    relayout(0)
    adds[1].wait_recv()
    rep_send[2] = rep_send[1] + rep_recv[1]
    adds[2].start()
    collect(1)
    relayout(1)

    with_tokens = dot(stack[STACK:ALL, :], across[...], NN)
    for j in range(STACK // 128):
        proj[j] = with_tokens[:, j * 128 : (j + 1) * 128]
    proj[STACK // 128] = dot(stack[STACK:ALL, :], stack[STACK:ALL, :], NT)

    def rows_of(kind, layer, cols):
        return jnp.concatenate(
            [
                jnp.concatenate([proj[j, pl.ds(hc * 32 + kind * 16 + layer, 8, stride=2), :] for hc in range(4)], axis=0)
                for j in cols
            ],
            axis=1,
        )

    tokens, grads, units = (0, 1), (2, 3), (4,)
    in_scale = D ** (-0.5)
    out_scale = H ** (-0.5)

    def put(kind, layer, v):
        expand[...] = jnp.zeros_like(expand)
        for j in range(2):
            for hc in range(4):
                expand[j, pl.ds(hc * 32 + kind * 16 + layer, 8, stride=2), :] = v[
                    hc * 8 : hc * 8 + 8, j * 128 : (j + 1) * 128
                ]
        return jnp.concatenate([expand[0], expand[1]], axis=1).astype(BF16)

    ss0 = ss[...]
    inv0 = lax.rsqrt(ss0 * (1.0 / D) + norm_eps)
    pre0 = rows_of(0, 0, tokens) * (inv0 * in_scale)
    sig0 = jax.nn.sigmoid(pre0)
    act0 = pre0 * sig0 * out_scale
    out0_h = rows_of(1, 0, tokens)
    gram = jnp.concatenate([rows_of(0, 1, units), rows_of(1, 0, units)], axis=0).astype(BF16)
    act_e = put(1, 0, act0)
    mixed = dot(gram, act_e, NN)
    in1_h1 = rows_of(0, 1, tokens) + mixed[0:H]
    out0_h1 = out0_h + mixed[H : 2 * H]
    ss1 = ss0 + jnp.sum(act0 * (out0_h + out0_h1), axis=0, keepdims=True)
    inv1 = lax.rsqrt(jnp.maximum(ss1, 0.0) * (1.0 / D) + norm_eps)
    pre1 = in1_h1 * (inv1 * in_scale)
    sig1 = jax.nn.sigmoid(pre1)
    act1 = pre1 * sig1 * out_scale
    grad_pre1 = rows_of(1, 1, grads) * out_scale * sig1 * (1.0 + pre1 * (1.0 - sig1))
    back = grad_pre1 * (inv1 * in_scale)
    pull = (inv1 * inv1 * (1.0 / D)) * jnp.sum(back * in1_h1, axis=0, keepdims=True)
    back_e = put(0, 1, back)
    grad_act0 = rows_of(1, 0, grads) + dot(gram[H : 2 * H], back_e, NN) - pull * out0_h1
    grad_pre0 = grad_act0 * out_scale * sig0 * (1.0 + pre0 * (1.0 - sig0))

    act0_b = act0.astype(BF16)
    pulled = act0 * pull
    mix1 = dot(back.astype(BF16), act_e, NT)
    mix0 = dot(act0_b, back_e, NT) - dot(pulled.astype(BF16), act_e, NT)
    zero = jnp.zeros((H, CHIP), F32)
    zero_u = jnp.zeros((H, 4 * H), F32)
    for kind, layer, parts in (
        (0, 0, (grad_pre0 * (inv0 * in_scale), zero, zero_u)),
        (0, 1, (back, zero, mix1)),
        (1, 0, (-pulled, act0, mix0)),
        (1, 1, (zero, act1, zero_u)),
    ):
        for h in range(2):
            for part, cols in zip(parts, (tokens, grads, units), strict=True):
                for i, j in enumerate(cols):
                    coef[j, pl.ds(h * 32 + kind * 16 + layer, 8, stride=2), :] = part[
                        h * 16 : h * 16 + 8, i * 128 : (i + 1) * 128
                    ]

    def gradients(h):
        weights = jnp.concatenate(
            [coef[j, pl.ds(pl.multiple_of(h * 32, 32), 32), :] for j in range(ALL // 128)], axis=1
        ).astype(BF16)
        for part in range(2):
            first = part * (ROWS // 2)
            out = dot(weights, stack[:, first * 128 : (first + ROWS // 2) * 128], NN).astype(BF16)
            for j in range(ROWS // 2):
                send[h, :, first + j] = out[:, j * 128 : (j + 1) * 128].reshape(PLANE, 2, 128)
            rows = pl.ds(first, ROWS // 2)

            def out_one(k, _, rows=rows):
                q = peer(k)
                remote(
                    send.at[h, q, rows], recv.at[h, place, rows], red_send.at[h], red_recv.at[h], in_plane(q)
                ).start()
                return 0

            lax.fori_loop(1, PLANE, out_one, 0)
        recv[h, place] = send[h, place]

    def summed(h):
        pltpu.make_async_copy(
            recv.at[h, pl.ds(0, PLANE - 1)], recv.at[h, pl.ds(0, PLANE - 1)], red_recv.at[h]
        ).wait()
        total = recv[h, 0].reshape(2 * ROWS, 128).astype(F32)
        for q in range(1, PLANE):
            total += recv[h, q].reshape(2 * ROWS, 128).astype(F32)
        return total

    gradients(1)
    gradients(0)
    z_send[...] = summed(1).astype(BF16).reshape(ROWS, 2, 128)
    z_back = remote(z_send, z_recv, z_back_sems.at[0], z_back_sems.at[1], other_z)
    z_back.start()

    for load in (loads[3], loads[4], loads[6]):
        load.wait()
    adds[2].wait_recv()
    total = rep_send[2] + rep_recv[2]
    anchor = an[...]
    delta = total * (1.0 / REPS)
    velocity = outer_beta * mo[...] + delta
    new_anchor = anchor - outer_rate * (delta + outer_beta * velocity)
    new_m[...] = velocity
    new_a[...] = new_anchor

    own = summed(0)
    z_back.wait_recv()
    flat[...] = (own + z_recv[...].reshape(2 * ROWS, 128).astype(F32)) * (1.0 / (TOK * 64))
    count = jnp.full((8, 128), step.astype(F32), F32)
    correct_one = (1.0 - jnp.exp(count * math.log(beta_one)))[0:1]
    correct_two = (1.0 - jnp.exp(count * math.log(beta_two)))[0:1]
    for layer in range(2):
        gradient = flat[pl.ds(layer, ROWS, stride=2), :]
        params = w_own[layer]
        one = beta_one * fm[layer] + (1.0 - beta_one) * gradient
        two = beta_two * sm[layer] + (1.0 - beta_two) * gradient * gradient
        updated = params - inner_rate * (
            one / correct_one / (jnp.sqrt(two / correct_two) + adam_eps) + decay_rate * params
        )
        merged = mixing * updated + (1.0 - mixing) * new_anchor
        here = chosen if layer == 1 else 1.0 - chosen
        new_w[0, layer] = jnp.where(jnp.full((ROWS, 128), here, F32) > 0.5, merged, updated)

    @pl.when(late)
    def _():
        z_copy.wait_send()

    @pl.when(early & (core == 0))
    def _():
        for copy in hops()[1]:
            copy.wait_send()

    for copy in [pair, z_back, *tok_copies, *adds]:
        copy.wait_send()
    for h in range(2):
        most = w_all.at[h, 0, pl.ds(0, PLANE - 1)]
        pltpu.make_async_copy(most, most, ring_send.at[h]).wait()
        most = w_all.at[h, 0, pl.ds(0, PLANE - 1 + h)]
        pltpu.make_async_copy(most, most, fwd_send.at[h]).wait()
        most = send.at[h, pl.ds(0, PLANE - 1)]
        pltpu.make_async_copy(most, most, red_send.at[h]).wait()


def place_results(a, b, c, to_a, to_b, to_c):
    to_a[...] = a[...]
    to_b[...] = b[...]
    to_c[...] = c[...]


def shards(inputs, cotangent, weights, first_moment, second_moment, anchor, momentum, fragment):
    hbm = pl.BlockSpec(memory_space=pltpu.HBM)
    vmem = pl.BlockSpec(memory_space=pltpu.VMEM)
    dma = pltpu.SemaphoreType.DMA
    unit = (ROWS, 2, 128)
    results = pl.pallas_call(
        kernel,
        out_shape=(
            pltpu.VMEM((1, 2, ROWS, 128), F32),
            pltpu.VMEM((ROWS, 128), F32),
            pltpu.VMEM((ROWS, 128), F32),
        ),
        in_specs=[hbm] * 8,
        out_specs=(vmem, vmem, vmem),
        scratch_shapes=[
            pltpu.VMEM((ALL, D), BF16),
            pltpu.VMEM((D, STACK), BF16),
            pltpu.VMEM((2, 2, PLANE) + unit, BF16),
            pltpu.VMEM((2, PLANE) + unit, BF16),
            pltpu.VMEM((2, PLANE) + unit, BF16),
            pltpu.VMEM(unit, BF16),
            pltpu.VMEM(unit, BF16),
            pltpu.VMEM((2,) + unit, BF16),
            pltpu.VMEM((2, ROWS, 128), F32),
            pltpu.VMEM((2, ROWS, 128), F32),
            pltpu.VMEM((2, ROWS, 128), F32),
            pltpu.VMEM((ROWS, 128), F32),
            pltpu.VMEM((ROWS, 128), F32),
            pltpu.VMEM((3, ROWS, 128), F32),
            pltpu.VMEM((3, ROWS, 128), F32),
            pltpu.VMEM((ALL // 128, 4 * H, 128), F32),
            pltpu.VMEM((ALL // 128, 2 * H, 128), F32),
            pltpu.VMEM((2, 4 * H, 128), F32),
            pltpu.VMEM((2 * ROWS, 128), F32),
            pltpu.VMEM((1, CHIP), F32),
            pltpu.SMEM((1,), jnp.int32),
            dma((8,)),
            dma((2,)),
            dma((2,)),
            dma((2,)),
            dma((2,)),
            dma((2, PLANE)),
            dma((2,)),
            dma((2,)),
            dma((2,)),
            dma((2,)),
            dma((2,)),
            dma((2,)),
            dma((3,)),
            dma((3,)),
            dma((2,)),
            dma((2,)),
            dma((2,)),
            pltpu.SemaphoreType.REGULAR,
            pltpu.SemaphoreType.REGULAR,
        ],
        compiler_params=pltpu.CompilerParams(
            collective_id=0, has_side_effects=True, vmem_limit_bytes=56 * 1024 * 1024
        ),
        name="window",
    )(inputs, cotangent, weights, first_moment, second_moment, anchor, momentum, fragment)
    return pl.pallas_call(
        place_results,
        out_shape=tuple(jax.ShapeDtypeStruct(r.shape, r.dtype) for r in results),
        in_specs=[vmem] * 3,
        out_specs=(vmem,) * 3,
        name="results",
    )(*(pltpu.with_memory_space_constraint(r, pltpu.VMEM) for r in results))


def solution(mesh):
    placed = (
        P("rep", "fsdp", None),
        P("rep", "fsdp", None),
        P("rep", None, "fsdp", None),
        P("rep", None, "fsdp", None),
        P("rep", None, "fsdp", None),
        P("fsdp", None),
        P("fsdp", None),
        P(),
    )
    return jax.shard_map(
        shards,
        mesh=mesh,
        in_specs=placed,
        out_specs=(P("rep", None, "fsdp", None), P("fsdp", None), P("fsdp", None)),
        check_vma=False,
    )
```

```python
import math

import jax
import jax.numpy as jnp
from jax import lax
from jax.experimental import pallas as pl
from jax.experimental.pallas import tpu as pltpu
from jax.sharding import PartitionSpec as P

norm_eps = 1e-05
beta_one = 0.9
beta_two = 0.95
adam_eps = 1e-08
decay_rate = 0.1
inner_rate = 0.05
outer_rate = 0.7
outer_beta = 0.9
mixing = 0.5

MESH = pl.DeviceIdType.MESH
TOK = 128
D = 7168
H = 32
ROWS = 56
PLANE = 16
REPS = 8
F32 = jnp.float32
BF16 = jnp.bfloat16
CHIP = 2 * TOK
GRADS = CHIP
STACK = 2 * CHIP
ALL = STACK + 4 * H

NT = (((1,), (1,)), ((), ()))
NN = (((1,), (0,)), ((), ()))


def dot(a, b, dims):
    return lax.dot_general(a, b, dims, preferred_element_type=F32)


def kernel(
    x_h, g_h, w_h, fm_h, sm_h, an_h, mo_h, fr_h,
    new_w, new_a, new_m,
    stack, across, w_all, send, recv, z_send, z_recv, staged, w_own, fm, sm, an, mo, rep_send, rep_recv,
    proj, coef, expand, flat, ss,
    step_s, load_sem, z_sems, z_back_sems, ring_send, ring_recv, fwd_send, fwd_recv, tok_send, tok_recv,
    red_send, red_recv, rep_out, rep_in, there, ready,
):
    rep = lax.axis_index("rep")
    fsdp = lax.axis_index("fsdp")
    place = fsdp // 4
    zh = (fsdp // 2) % 2
    core = fsdp % 2

    def peer(k):
        return lax.rem(place + k, PLANE)

    def in_plane(q):
        return (rep, q * 4 + zh * 2 + core)

    early = zh == 0
    late = zh == 1
    other_z = (rep, place * 4 + (1 - zh) * 2 + core)
    sibling = (rep, place * 4 + zh * 2 + (1 - core))
    across_rep = (
        lax.rem(rep + 4, REPS),
        rep + 2 - 4 * lax.rem(rep // 2, 2),
        rep + 1 - 2 * lax.rem(rep, 2),
    )

    def remote(src, dst, ssem, rsem, device):
        return pltpu.make_async_remote_copy(
            src_ref=src, dst_ref=dst, send_sem=ssem, recv_sem=rsem, device_id=device, device_id_type=MESH
        )

    barrier = pltpu.get_barrier_semaphore()

    def greet(device):
        pl.semaphore_signal(barrier, inc=1, device_id=device, device_id_type=MESH)

    over = (rep, fsdp - core + 2 - 4 * zh)
    over_staged = (across_rep[0], fsdp - core + 2 - 4 * zh)

    @pl.when(early & (core == 0))
    def _():
        greet((across_rep[0], fsdp))
        greet(over)

    @pl.when(early & (core == 1))
    def _():
        greet((rep, fsdp + 2))

    @pl.when(early)
    def _():
        greet(over_staged)

    @pl.when(late & (core == 1))
    def _():
        greet(sibling)

    for r in across_rep:
        greet((r, place * 4 + zh * 2 + 1))

    @pl.when(core == 0)
    def _():
        greet(sibling)

    def greet_plane(k, _):
        greet((rep, peer(k) * 4 + zh * 2 + 1))
        return 0

    lax.fori_loop(1, PLANE, greet_plane, 0)

    loads = [
        pltpu.make_async_copy(src, dst, load_sem.at[i])
        for i, (src, dst) in enumerate(
            [
                (w_h.at[0], w_own),
                (x_h.at[0], stack.at[pl.ds(0, TOK)]),
                (g_h.at[0], stack.at[pl.ds(GRADS, TOK)]),
                (fm_h.at[0], fm),
                (sm_h.at[0], sm),
                (an_h, an),
                (mo_h, mo),
                (fr_h, step_s),
            ]
        )
    ]
    for load in loads:
        load.start()
    @pl.when(late & (core == 0))
    def _():
        pl.semaphore_wait(barrier, 4)
        for c in range(2):
            pl.semaphore_signal(there, inc=1, device_id=(across_rep[0], fsdp - 2 + c), device_id_type=MESH)

    loads[0].wait()
    flat[pl.ds(0, ROWS, stride=2), :] = w_own[0]
    flat[pl.ds(1, ROWS, stride=2), :] = w_own[1]
    w_all[0, 0, place] = flat[...].astype(BF16).reshape(ROWS, 2, 128)
    own = w_all.at[0, 0, place]
    z_copy = remote(own, w_all.at[1, 0, place], z_sems.at[0], z_sems.at[1], other_z)
    half = remote(own, staged, z_sems.at[2], z_sems.at[3], (across_rep[0], fsdp))
    rest = remote(staged, w_all.at[1, 0, place], z_sems.at[0], z_sems.at[1], (across_rep[0], fsdp + 2 - 4 * zh))

    @pl.when(early & (core == 0))
    def _():
        pl.semaphore_wait(barrier, 1)
        half.start()

    @pl.when(late & (core == 0))
    def _():
        z_copy.start()

    loads[7].wait()
    step = step_s[0]
    chosen = lax.rem(step, 2).astype(F32)
    loads[5].wait()
    rep_send[0] = an[...] - (w_own[0] * (1.0 - chosen) + w_own[1] * chosen)

    def turn(start):
        def one(r, _):
            at = pl.multiple_of(r * 128, 128)
            across[pl.ds(at, 128), start : start + TOK] = stack[pl.ds(start, TOK), pl.ds(at, 128)].T
            return 0

        lax.fori_loop(0, ROWS, one, 0, unroll=14)

    loads[1].wait()
    turn(0)
    loads[2].wait()
    turn(GRADS)

    @pl.when(core == 1)
    def _():
        pl.semaphore_wait(barrier, 2 * PLANE - 1 + 2 * len(across_rep) + zh)
        pl.semaphore_signal(ready, inc=1, device_id=sibling, device_id_type=MESH)

    @pl.when(core == 0)
    def _():
        pl.semaphore_wait(ready, 1)

    @pl.when(early & (core == 1))
    def _():
        half.start()

    @pl.when(late & (core == 1))
    def _():
        z_copy.start()

    def spread(h):
        def one(k, _):
            remote(
                w_all.at[h, 0, place], w_all.at[h, 0, place], ring_send.at[h], ring_recv.at[h, place], in_plane(peer(k))
            ).start()
            return 0

        lax.fori_loop(1, PLANE, one, 0)

    def hand_on(h, q):
        remote(w_all.at[h, 0, q], w_all.at[h, 1, q], fwd_send.at[h], fwd_recv.at[h], sibling).start()

    def collect(h):
        def one(k, _):
            q = lax.rem(place + PLANE - k, PLANE)
            remote(
                w_all.at[h, 0, q], w_all.at[h, 0, q], ring_send.at[h], ring_recv.at[h, q], in_plane(q)
            ).wait_recv()
            hand_on(h, q)
            return 0

        lax.fori_loop(1, PLANE, one, 0)

    @pl.when(early)
    def _():
        half.wait_recv()
        pl.semaphore_wait(there, 1)
        rest.start()

    spread(0)
    hand_on(0, place)
    tok_copies = []
    for i, start in enumerate((0, GRADS)):
        copy = remote(
            stack.at[pl.ds(start, TOK)], stack.at[pl.ds(start + TOK, TOK)], tok_send.at[i], tok_recv.at[i], sibling
        )
        tok_copies.append(copy)

    adds = [
        remote(rep_send.at[i], rep_recv.at[i], rep_out.at[i], rep_in.at[i], (across_rep[i], fsdp)) for i in range(3)
    ]

    for copy in tok_copies:
        copy.start()
    adds[0].start()

    z_copy.wait_recv()
    spread(1)
    hand_on(1, place)

    adds[0].wait_recv()
    rep_send[1] = rep_send[0] + rep_recv[0]
    adds[1].start()

    def relayout(h):
        most = w_all.at[h, 1]
        remote(most, most, fwd_send.at[h], fwd_recv.at[h], sibling).wait_recv()

        def one(r, _):
            at = pl.multiple_of(r * 128, 128)
            for c in range(2):
                stack[pl.ds(STACK + h * 64 + c * 32, 32), pl.ds(at, 128)] = w_all[h, c, :, r].reshape(32, 128)
            return 0

        lax.fori_loop(0, ROWS, one, 0, unroll=8)

    for copy, start in zip(tok_copies, (TOK, GRADS + TOK), strict=True):
        copy.wait_recv()
        turn(start)

    def square(r, acc):
        v = across[pl.ds(pl.multiple_of(r * 128, 128), 128), 0:CHIP].astype(F32)
        v = v * v
        for i in range(16):
            acc += v[i * 8 : i * 8 + 8]
        return acc

    acc = lax.fori_loop(0, ROWS, square, jnp.zeros((8, CHIP), F32), unroll=4)
    ss[...] = jnp.sum(acc, axis=0, keepdims=True)

    collect(0)
    relayout(0)
    adds[1].wait_recv()
    rep_send[2] = rep_send[1] + rep_recv[1]
    adds[2].start()
    collect(1)
    relayout(1)

    with_tokens = dot(stack[STACK:ALL, :], across[...], NN)
    for j in range(STACK // 128):
        proj[j] = with_tokens[:, j * 128 : (j + 1) * 128]
    proj[STACK // 128] = dot(stack[STACK:ALL, :], stack[STACK:ALL, :], NT)

    def rows_of(kind, layer, cols):
        return jnp.concatenate(
            [
                jnp.concatenate([proj[j, pl.ds(hc * 32 + kind * 16 + layer, 8, stride=2), :] for hc in range(4)], axis=0)
                for j in cols
            ],
            axis=1,
        )

    tokens, grads, units = (0, 1), (2, 3), (4,)
    in_scale = D ** (-0.5)
    out_scale = H ** (-0.5)

    def put(kind, layer, v):
        expand[...] = jnp.zeros_like(expand)
        for j in range(2):
            for hc in range(4):
                expand[j, pl.ds(hc * 32 + kind * 16 + layer, 8, stride=2), :] = v[
                    hc * 8 : hc * 8 + 8, j * 128 : (j + 1) * 128
                ]
        return jnp.concatenate([expand[0], expand[1]], axis=1).astype(BF16)

    ss0 = ss[...]
    inv0 = lax.rsqrt(ss0 * (1.0 / D) + norm_eps)
    pre0 = rows_of(0, 0, tokens) * (inv0 * in_scale)
    sig0 = jax.nn.sigmoid(pre0)
    act0 = pre0 * sig0 * out_scale
    out0_h = rows_of(1, 0, tokens)
    gram = jnp.concatenate([rows_of(0, 1, units), rows_of(1, 0, units)], axis=0).astype(BF16)
    act_e = put(1, 0, act0)
    mixed = dot(gram, act_e, NN)
    in1_h1 = rows_of(0, 1, tokens) + mixed[0:H]
    out0_h1 = out0_h + mixed[H : 2 * H]
    ss1 = ss0 + jnp.sum(act0 * (out0_h + out0_h1), axis=0, keepdims=True)
    inv1 = lax.rsqrt(jnp.maximum(ss1, 0.0) * (1.0 / D) + norm_eps)
    pre1 = in1_h1 * (inv1 * in_scale)
    sig1 = jax.nn.sigmoid(pre1)
    act1 = pre1 * sig1 * out_scale
    grad_pre1 = rows_of(1, 1, grads) * out_scale * sig1 * (1.0 + pre1 * (1.0 - sig1))
    back = grad_pre1 * (inv1 * in_scale)
    pull = (inv1 * inv1 * (1.0 / D)) * jnp.sum(back * in1_h1, axis=0, keepdims=True)
    back_e = put(0, 1, back)
    grad_act0 = rows_of(1, 0, grads) + dot(gram[H : 2 * H], back_e, NN) - pull * out0_h1
    grad_pre0 = grad_act0 * out_scale * sig0 * (1.0 + pre0 * (1.0 - sig0))

    act0_b = act0.astype(BF16)
    pulled = act0 * pull
    mix1 = dot(back.astype(BF16), act_e, NT)
    mix0 = dot(act0_b, back_e, NT) - dot(pulled.astype(BF16), act_e, NT)
    zero = jnp.zeros((H, CHIP), F32)
    zero_u = jnp.zeros((H, 4 * H), F32)
    for kind, layer, parts in (
        (0, 0, (grad_pre0 * (inv0 * in_scale), zero, zero_u)),
        (0, 1, (back, zero, mix1)),
        (1, 0, (-pulled, act0, mix0)),
        (1, 1, (zero, act1, zero_u)),
    ):
        for h in range(2):
            for part, cols in zip(parts, (tokens, grads, units), strict=True):
                for i, j in enumerate(cols):
                    coef[j, pl.ds(h * 32 + kind * 16 + layer, 8, stride=2), :] = part[
                        h * 16 : h * 16 + 8, i * 128 : (i + 1) * 128
                    ]

    def gradients(h):
        weights = jnp.concatenate(
            [coef[j, pl.ds(pl.multiple_of(h * 32, 32), 32), :] for j in range(ALL // 128)], axis=1
        ).astype(BF16)
        for part in range(2):
            first = part * (ROWS // 2)
            out = dot(weights, stack[:, first * 128 : (first + ROWS // 2) * 128], NN).astype(BF16)
            for j in range(ROWS // 2):
                send[h, :, first + j] = out[:, j * 128 : (j + 1) * 128].reshape(PLANE, 2, 128)
            rows = pl.ds(first, ROWS // 2)

            def out_one(k, _, rows=rows):
                q = peer(k)
                remote(
                    send.at[h, q, rows], recv.at[h, place, rows], red_send.at[h], red_recv.at[h], in_plane(q)
                ).start()
                return 0

            lax.fori_loop(1, PLANE, out_one, 0)
        recv[h, place] = send[h, place]

    def summed(h):
        pltpu.make_async_copy(
            recv.at[h, pl.ds(0, PLANE - 1)], recv.at[h, pl.ds(0, PLANE - 1)], red_recv.at[h]
        ).wait()
        total = recv[h, 0].reshape(2 * ROWS, 128).astype(F32)
        for q in range(1, PLANE):
            total += recv[h, q].reshape(2 * ROWS, 128).astype(F32)
        return total

    gradients(1)
    gradients(0)
    z_send[...] = summed(1).astype(BF16).reshape(ROWS, 2, 128)
    z_back = remote(z_send, z_recv, z_back_sems.at[0], z_back_sems.at[1], other_z)
    z_back.start()

    for load in (loads[3], loads[4], loads[6]):
        load.wait()
    adds[2].wait_recv()
    total = rep_send[2] + rep_recv[2]
    anchor = an[...]
    delta = total * (1.0 / REPS)
    velocity = outer_beta * mo[...] + delta
    new_anchor = anchor - outer_rate * (delta + outer_beta * velocity)
    new_m[...] = velocity
    new_a[...] = new_anchor

    mine = summed(0)
    z_back.wait_recv()
    flat[...] = (mine + z_recv[...].reshape(2 * ROWS, 128).astype(F32)) * (1.0 / (TOK * 64))
    count = jnp.full((8, 128), step.astype(F32), F32)
    correct_one = (1.0 - jnp.exp(count * math.log(beta_one)))[0:1]
    correct_two = (1.0 - jnp.exp(count * math.log(beta_two)))[0:1]
    for layer in range(2):
        gradient = flat[pl.ds(layer, ROWS, stride=2), :]
        params = w_own[layer]
        one = beta_one * fm[layer] + (1.0 - beta_one) * gradient
        two = beta_two * sm[layer] + (1.0 - beta_two) * gradient * gradient
        updated = params - inner_rate * (
            one / correct_one / (jnp.sqrt(two / correct_two) + adam_eps) + decay_rate * params
        )
        merged = mixing * updated + (1.0 - mixing) * new_anchor
        here = chosen if layer == 1 else 1.0 - chosen
        new_w[0, layer] = jnp.where(jnp.full((ROWS, 128), here, F32) > 0.5, merged, updated)

    @pl.when(early)
    def _():
        half.wait_send()

    z_copy.wait_send()
    for copy in [z_back, *tok_copies, *adds]:
        copy.wait_send()
    for h in range(2):
        most = w_all.at[h, 0, pl.ds(0, PLANE - 1)]
        pltpu.make_async_copy(most, most, ring_send.at[h]).wait()
        pltpu.make_async_copy(w_all.at[h, 0], w_all.at[h, 0], fwd_send.at[h]).wait()
        most = send.at[h, pl.ds(0, PLANE - 1)]
        pltpu.make_async_copy(most, most, red_send.at[h]).wait()


def place_results(a, b, c, to_a, to_b, to_c):
    to_a[...] = a[...]
    to_b[...] = b[...]
    to_c[...] = c[...]


def shards(inputs, cotangent, weights, first_moment, second_moment, anchor, momentum, fragment):
    hbm = pl.BlockSpec(memory_space=pltpu.HBM)
    vmem = pl.BlockSpec(memory_space=pltpu.VMEM)
    dma = pltpu.SemaphoreType.DMA
    unit = (ROWS, 2, 128)
    results = pl.pallas_call(
        kernel,
        out_shape=(
            pltpu.VMEM((1, 2, ROWS, 128), F32),
            pltpu.VMEM((ROWS, 128), F32),
            pltpu.VMEM((ROWS, 128), F32),
        ),
        in_specs=[hbm] * 8,
        out_specs=(vmem, vmem, vmem),
        scratch_shapes=[
            pltpu.VMEM((ALL, D), BF16),
            pltpu.VMEM((D, STACK), BF16),
            pltpu.VMEM((2, 2, PLANE) + unit, BF16),
            pltpu.VMEM((2, PLANE) + unit, BF16),
            pltpu.VMEM((2, PLANE) + unit, BF16),
            pltpu.VMEM(unit, BF16),
            pltpu.VMEM(unit, BF16),
            pltpu.VMEM(unit, BF16),
            pltpu.VMEM((2, ROWS, 128), F32),
            pltpu.VMEM((2, ROWS, 128), F32),
            pltpu.VMEM((2, ROWS, 128), F32),
            pltpu.VMEM((ROWS, 128), F32),
            pltpu.VMEM((ROWS, 128), F32),
            pltpu.VMEM((3, ROWS, 128), F32),
            pltpu.VMEM((3, ROWS, 128), F32),
            pltpu.VMEM((ALL // 128, 4 * H, 128), F32),
            pltpu.VMEM((ALL // 128, 2 * H, 128), F32),
            pltpu.VMEM((2, 4 * H, 128), F32),
            pltpu.VMEM((2 * ROWS, 128), F32),
            pltpu.VMEM((1, CHIP), F32),
            pltpu.SMEM((1,), jnp.int32),
            dma((8,)),
            dma((4,)),
            dma((2,)),
            dma((2,)),
            dma((2, PLANE)),
            dma((2,)),
            dma((2,)),
            dma((2,)),
            dma((2,)),
            dma((2,)),
            dma((2,)),
            dma((3,)),
            dma((3,)),
            pltpu.SemaphoreType.REGULAR,
            pltpu.SemaphoreType.REGULAR,
        ],
        compiler_params=pltpu.CompilerParams(
            collective_id=0, has_side_effects=True, vmem_limit_bytes=56 * 1024 * 1024
        ),
        name="window",
    )(inputs, cotangent, weights, first_moment, second_moment, anchor, momentum, fragment)
    return pl.pallas_call(
        place_results,
        out_shape=tuple(jax.ShapeDtypeStruct(r.shape, r.dtype) for r in results),
        in_specs=[vmem] * 3,
        out_specs=(vmem,) * 3,
        name="results",
    )(*(pltpu.with_memory_space_constraint(r, pltpu.VMEM) for r in results))


def solution(mesh):
    placed = (
        P("rep", "fsdp", None),
        P("rep", "fsdp", None),
        P("rep", None, "fsdp", None),
        P("rep", None, "fsdp", None),
        P("rep", None, "fsdp", None),
        P("fsdp", None),
        P("fsdp", None),
        P(),
    )
    return jax.shard_map(
        shards,
        mesh=mesh,
        in_specs=placed,
        out_specs=(P("rep", None, "fsdp", None), P("fsdp", None), P("fsdp", None)),
        check_vma=False,
    )
```

```python
import math

import jax
import jax.numpy as jnp
from jax import lax
from jax.experimental import pallas as pl
from jax.experimental.pallas import tpu as pltpu
from jax.sharding import PartitionSpec as P

norm_eps = 1e-05
beta_one = 0.9
beta_two = 0.95
adam_eps = 1e-08
decay_rate = 0.1
inner_rate = 0.05
outer_rate = 0.7
outer_beta = 0.9
mixing = 0.5

MESH = pl.DeviceIdType.MESH
TOK = 128
D = 7168
H = 32
ROWS = 56
PLANE = 16
REPS = 8
F32 = jnp.float32
BF16 = jnp.bfloat16
CHIP = 2 * TOK
GRADS = CHIP
STACK = 2 * CHIP
ALL = STACK + 4 * H

NT = (((1,), (1,)), ((), ()))
NN = (((1,), (0,)), ((), ()))


def dot(a, b, dims):
    return lax.dot_general(a, b, dims, preferred_element_type=F32)


def kernel(
    x_h, g_h, w_h, fm_h, sm_h, an_h, mo_h, fr_h,
    new_w, new_a, new_m,
    stack, across, w_all, send, recv, z_send, z_recv, staged, w_own, fm, sm, an, mo, rep_send, rep_recv,
    proj, coef, expand, flat, ss,
    step_s, load_sem, z_sems, z_back_sems, ring_send, ring_recv, fwd_send, fwd_recv, tok_send, tok_recv,
    red_send, red_recv, rep_out, rep_in, there, ready,
):
    rep = lax.axis_index("rep")
    fsdp = lax.axis_index("fsdp")
    place = fsdp // 4
    zh = (fsdp // 2) % 2
    core = fsdp % 2

    def peer(k):
        return lax.rem(place + k, PLANE)

    def in_plane(q):
        return (rep, q * 4 + zh * 2 + core)

    early = zh == 0
    late = zh == 1
    other_z = (rep, place * 4 + (1 - zh) * 2 + core)
    sibling = (rep, place * 4 + zh * 2 + (1 - core))
    across_rep = (
        lax.rem(rep + 4, REPS),
        rep + 2 - 4 * lax.rem(rep // 2, 2),
        rep + 1 - 2 * lax.rem(rep, 2),
    )

    def remote(src, dst, ssem, rsem, device):
        return pltpu.make_async_remote_copy(
            src_ref=src, dst_ref=dst, send_sem=ssem, recv_sem=rsem, device_id=device, device_id_type=MESH
        )

    barrier = pltpu.get_barrier_semaphore()

    def greet(device):
        pl.semaphore_signal(barrier, inc=1, device_id=device, device_id_type=MESH)

    over = (rep, fsdp - core + 2 - 4 * zh)
    over_staged = (across_rep[0], fsdp - core + 2 - 4 * zh)

    @pl.when(early & (core == 0))
    def _():
        greet((across_rep[0], fsdp))
        greet(over)

    @pl.when(early & (core == 1))
    def _():
        greet((rep, fsdp + 2))

    @pl.when(early)
    def _():
        greet(over_staged)

    @pl.when(late & (core == 1))
    def _():
        greet(sibling)

    for r in across_rep:
        greet((r, place * 4 + zh * 2 + 1))

    @pl.when(core == 0)
    def _():
        greet(sibling)

    def greet_plane(k, _):
        greet((rep, peer(k) * 4 + zh * 2 + 1))
        return 0

    lax.fori_loop(1, PLANE, greet_plane, 0)

    loads = [
        pltpu.make_async_copy(src, dst, load_sem.at[i])
        for i, (src, dst) in enumerate(
            [
                (w_h.at[0], w_own),
                (x_h.at[0], stack.at[pl.ds(0, TOK)]),
                (g_h.at[0], stack.at[pl.ds(GRADS, TOK)]),
                (fm_h.at[0], fm),
                (sm_h.at[0], sm),
                (an_h, an),
                (mo_h, mo),
                (fr_h, step_s),
            ]
        )
    ]
    for load in loads:
        load.start()
    @pl.when(late & (core == 0))
    def _():
        pl.semaphore_wait(barrier, 4)
        for c in range(2):
            pl.semaphore_signal(there, inc=1, device_id=(across_rep[0], fsdp - 2 + c), device_id_type=MESH)

    loads[0].wait()
    flat[pl.ds(0, ROWS, stride=2), :] = w_own[0]
    flat[pl.ds(1, ROWS, stride=2), :] = w_own[1]
    w_all[0, 0, place] = flat[...].astype(BF16).reshape(ROWS, 2, 128)
    own = w_all.at[0, 0, place]
    z_copy = remote(own, w_all.at[1, 0, place], z_sems.at[0], z_sems.at[1], other_z)
    half = remote(own, staged, z_sems.at[2], z_sems.at[3], (across_rep[0], fsdp))
    rest = remote(staged, w_all.at[1, 0, place], z_sems.at[0], z_sems.at[1], (across_rep[0], fsdp + 2 - 4 * zh))

    @pl.when(early & (core == 0))
    def _():
        pl.semaphore_wait(barrier, 1)
        half.start()

    @pl.when(late & (core == 0))
    def _():
        z_copy.start()

    loads[7].wait()
    step = step_s[0]
    chosen = lax.rem(step, 2).astype(F32)
    loads[5].wait()
    rep_send[0] = an[...] - (w_own[0] * (1.0 - chosen) + w_own[1] * chosen)

    def turn(start):
        def one(r, _):
            at = pl.multiple_of(r * 128, 128)
            across[pl.ds(at, 128), start : start + TOK] = stack[pl.ds(start, TOK), pl.ds(at, 128)].T
            return 0

        lax.fori_loop(0, ROWS, one, 0, unroll=14)

    loads[1].wait()
    turn(0)
    loads[2].wait()
    turn(GRADS)

    @pl.when(core == 1)
    def _():
        pl.semaphore_wait(barrier, 2 * PLANE - 1 + 2 * len(across_rep) + zh)
        pl.semaphore_signal(ready, inc=1, device_id=sibling, device_id_type=MESH)

    @pl.when(core == 0)
    def _():
        pl.semaphore_wait(ready, 1)

    @pl.when(early & (core == 1))
    def _():
        half.start()

    @pl.when(late & (core == 1))
    def _():
        z_copy.start()

    def spread(h):
        def one(k, _):
            remote(
                w_all.at[h, 0, place], w_all.at[h, 0, place], ring_send.at[h], ring_recv.at[h, place], in_plane(peer(k))
            ).start()
            return 0

        lax.fori_loop(1, PLANE, one, 0)

    def hand_on(h, q):
        remote(w_all.at[h, 0, q], w_all.at[h, 1, q], fwd_send.at[h], fwd_recv.at[h], sibling).start()

    def collect(h):
        def one(k, _):
            q = lax.rem(place + PLANE - k, PLANE)
            remote(
                w_all.at[h, 0, q], w_all.at[h, 0, q], ring_send.at[h], ring_recv.at[h, q], in_plane(q)
            ).wait_recv()
            hand_on(h, q)
            return 0

        lax.fori_loop(1, PLANE, one, 0)

    @pl.when(early)
    def _():
        half.wait_recv()
        pl.semaphore_wait(there, 1)
        rest.start()

    spread(0)
    hand_on(0, place)
    tok_copies = []
    for i, start in enumerate((0, GRADS)):
        copy = remote(
            stack.at[pl.ds(start, TOK)], stack.at[pl.ds(start + TOK, TOK)], tok_send.at[i], tok_recv.at[i], sibling
        )
        tok_copies.append(copy)

    adds = [
        remote(rep_send.at[i], rep_recv.at[i], rep_out.at[i], rep_in.at[i], (across_rep[i], fsdp)) for i in range(3)
    ]

    for copy in tok_copies:
        copy.start()
    adds[0].start()

    z_copy.wait_recv()
    spread(1)
    hand_on(1, place)

    adds[0].wait_recv()
    rep_send[1] = rep_send[0] + rep_recv[0]
    adds[1].start()

    def relayout(h):
        most = w_all.at[h, 1]
        remote(most, most, fwd_send.at[h], fwd_recv.at[h], sibling).wait_recv()

        def one(r, _):
            at = pl.multiple_of(r * 128, 128)
            for c in range(2):
                stack[pl.ds(STACK + h * 64 + c * 32, 32), pl.ds(at, 128)] = w_all[h, c, :, r].reshape(32, 128)
            return 0

        lax.fori_loop(0, ROWS, one, 0, unroll=8)

    for copy, start in zip(tok_copies, (TOK, GRADS + TOK), strict=True):
        copy.wait_recv()
        turn(start)

    def square(r, acc):
        v = across[pl.ds(pl.multiple_of(r * 128, 128), 128), 0:CHIP].astype(F32)
        v = v * v
        for i in range(16):
            acc += v[i * 8 : i * 8 + 8]
        return acc

    acc = lax.fori_loop(0, ROWS, square, jnp.zeros((8, CHIP), F32), unroll=4)
    ss[...] = jnp.sum(acc, axis=0, keepdims=True)

    collect(0)
    relayout(0)
    adds[1].wait_recv()
    rep_send[2] = rep_send[1] + rep_recv[1]
    adds[2].start()
    collect(1)
    relayout(1)

    with_tokens = dot(stack[STACK:ALL, :], across[...], NN)
    for j in range(STACK // 128):
        proj[j] = with_tokens[:, j * 128 : (j + 1) * 128]
    proj[STACK // 128] = dot(stack[STACK:ALL, :], stack[STACK:ALL, :], NT)

    def rows_of(kind, layer, cols):
        return jnp.concatenate(
            [
                jnp.concatenate([proj[j, pl.ds(hc * 32 + kind * 16 + layer, 8, stride=2), :] for hc in range(4)], axis=0)
                for j in cols
            ],
            axis=1,
        )

    tokens, grads, units = (0, 1), (2, 3), (4,)
    in_scale = D ** (-0.5)
    out_scale = H ** (-0.5)

    def put(kind, layer, v):
        expand[...] = jnp.zeros_like(expand)
        for j in range(2):
            for hc in range(4):
                expand[j, pl.ds(hc * 32 + kind * 16 + layer, 8, stride=2), :] = v[
                    hc * 8 : hc * 8 + 8, j * 128 : (j + 1) * 128
                ]
        return jnp.concatenate([expand[0], expand[1]], axis=1).astype(BF16)

    ss0 = ss[...]
    inv0 = lax.rsqrt(ss0 * (1.0 / D) + norm_eps)
    pre0 = rows_of(0, 0, tokens) * (inv0 * in_scale)
    sig0 = jax.nn.sigmoid(pre0)
    act0 = pre0 * sig0 * out_scale
    out0_h = rows_of(1, 0, tokens)
    gram = jnp.concatenate([rows_of(0, 1, units), rows_of(1, 0, units)], axis=0).astype(BF16)
    act_e = put(1, 0, act0)
    mixed = dot(gram, act_e, NN)
    in1_h1 = rows_of(0, 1, tokens) + mixed[0:H]
    out0_h1 = out0_h + mixed[H : 2 * H]
    ss1 = ss0 + jnp.sum(act0 * (out0_h + out0_h1), axis=0, keepdims=True)
    inv1 = lax.rsqrt(jnp.maximum(ss1, 0.0) * (1.0 / D) + norm_eps)
    pre1 = in1_h1 * (inv1 * in_scale)
    sig1 = jax.nn.sigmoid(pre1)
    act1 = pre1 * sig1 * out_scale
    grad_pre1 = rows_of(1, 1, grads) * out_scale * sig1 * (1.0 + pre1 * (1.0 - sig1))
    back = grad_pre1 * (inv1 * in_scale)
    pull = (inv1 * inv1 * (1.0 / D)) * jnp.sum(back * in1_h1, axis=0, keepdims=True)
    back_e = put(0, 1, back)
    grad_act0 = rows_of(1, 0, grads) + dot(gram[H : 2 * H], back_e, NN) - pull * out0_h1
    grad_pre0 = grad_act0 * out_scale * sig0 * (1.0 + pre0 * (1.0 - sig0))

    act0_b = act0.astype(BF16)
    pulled = act0 * pull
    mix1 = dot(back.astype(BF16), act_e, NT)
    mix0 = dot(act0_b, back_e, NT) - dot(pulled.astype(BF16), act_e, NT)
    zero = jnp.zeros((H, CHIP), F32)
    zero_u = jnp.zeros((H, 4 * H), F32)
    for kind, layer, parts in (
        (0, 0, (grad_pre0 * (inv0 * in_scale), zero, zero_u)),
        (0, 1, (back, zero, mix1)),
        (1, 0, (-pulled, act0, mix0)),
        (1, 1, (zero, act1, zero_u)),
    ):
        for h in range(2):
            for part, cols in zip(parts, (tokens, grads, units), strict=True):
                for i, j in enumerate(cols):
                    coef[j, pl.ds(h * 32 + kind * 16 + layer, 8, stride=2), :] = part[
                        h * 16 : h * 16 + 8, i * 128 : (i + 1) * 128
                    ]

    def gradients(h):
        weights = jnp.concatenate(
            [coef[j, pl.ds(pl.multiple_of(h * 32, 32), 32), :] for j in range(ALL // 128)], axis=1
        ).astype(BF16)
        for part in range(4):
            first = part * (ROWS // 4)
            out = dot(weights, stack[:, first * 128 : (first + ROWS // 4) * 128], NN).astype(BF16)
            for j in range(ROWS // 4):
                send[h, :, first + j] = out[:, j * 128 : (j + 1) * 128].reshape(PLANE, 2, 128)
            rows = pl.ds(first, ROWS // 4)

            def out_one(k, _, rows=rows):
                q = peer(k)
                remote(
                    send.at[h, q, rows], recv.at[h, place, rows], red_send.at[h], red_recv.at[h], in_plane(q)
                ).start()
                return 0

            lax.fori_loop(1, PLANE, out_one, 0)
        recv[h, place] = send[h, place]

    def summed(h):
        pltpu.make_async_copy(
            recv.at[h, pl.ds(0, PLANE - 1)], recv.at[h, pl.ds(0, PLANE - 1)], red_recv.at[h]
        ).wait()
        total = recv[h, 0].reshape(2 * ROWS, 128).astype(F32)
        for q in range(1, PLANE):
            total += recv[h, q].reshape(2 * ROWS, 128).astype(F32)
        return total

    gradients(1)

    @pl.when(early)
    def _():
        gradients(0)

    z_send[...] = summed(1).astype(BF16).reshape(ROWS, 2, 128)
    z_back = remote(z_send, z_recv, z_back_sems.at[0], z_back_sems.at[1], other_z)
    z_back.start()

    @pl.when(late)
    def _():
        gradients(0)


    for load in (loads[3], loads[4], loads[6]):
        load.wait()
    adds[2].wait_recv()
    total = rep_send[2] + rep_recv[2]
    anchor = an[...]
    delta = total * (1.0 / REPS)
    velocity = outer_beta * mo[...] + delta
    new_anchor = anchor - outer_rate * (delta + outer_beta * velocity)
    new_m[...] = velocity
    new_a[...] = new_anchor

    mine = summed(0)
    z_back.wait_recv()
    flat[...] = (mine + z_recv[...].reshape(2 * ROWS, 128).astype(F32)) * (1.0 / (TOK * 64))
    count = jnp.full((8, 128), step.astype(F32), F32)
    correct_one = (1.0 - jnp.exp(count * math.log(beta_one)))[0:1]
    correct_two = (1.0 - jnp.exp(count * math.log(beta_two)))[0:1]
    for layer in range(2):
        gradient = flat[pl.ds(layer, ROWS, stride=2), :]
        params = w_own[layer]
        one = beta_one * fm[layer] + (1.0 - beta_one) * gradient
        two = beta_two * sm[layer] + (1.0 - beta_two) * gradient * gradient
        updated = params - inner_rate * (
            one / correct_one / (jnp.sqrt(two / correct_two) + adam_eps) + decay_rate * params
        )
        merged = mixing * updated + (1.0 - mixing) * new_anchor
        here = chosen if layer == 1 else 1.0 - chosen
        new_w[0, layer] = jnp.where(jnp.full((ROWS, 128), here, F32) > 0.5, merged, updated)

    @pl.when(early)
    def _():
        half.wait_send()

    z_copy.wait_send()
    for copy in [z_back, *tok_copies, *adds]:
        copy.wait_send()
    for h in range(2):
        most = w_all.at[h, 0, pl.ds(0, PLANE - 1)]
        pltpu.make_async_copy(most, most, ring_send.at[h]).wait()
        pltpu.make_async_copy(w_all.at[h, 0], w_all.at[h, 0], fwd_send.at[h]).wait()
        most = send.at[h, pl.ds(0, PLANE - 1)]
        pltpu.make_async_copy(most, most, red_send.at[h]).wait()


def place_results(a, b, c, to_a, to_b, to_c):
    to_a[...] = a[...]
    to_b[...] = b[...]
    to_c[...] = c[...]


def shards(inputs, cotangent, weights, first_moment, second_moment, anchor, momentum, fragment):
    hbm = pl.BlockSpec(memory_space=pltpu.HBM)
    vmem = pl.BlockSpec(memory_space=pltpu.VMEM)
    dma = pltpu.SemaphoreType.DMA
    unit = (ROWS, 2, 128)
    results = pl.pallas_call(
        kernel,
        out_shape=(
            pltpu.VMEM((1, 2, ROWS, 128), F32),
            pltpu.VMEM((ROWS, 128), F32),
            pltpu.VMEM((ROWS, 128), F32),
        ),
        in_specs=[hbm] * 8,
        out_specs=(vmem, vmem, vmem),
        scratch_shapes=[
            pltpu.VMEM((ALL, D), BF16),
            pltpu.VMEM((D, STACK), BF16),
            pltpu.VMEM((2, 2, PLANE) + unit, BF16),
            pltpu.VMEM((2, PLANE) + unit, BF16),
            pltpu.VMEM((2, PLANE) + unit, BF16),
            pltpu.VMEM(unit, BF16),
            pltpu.VMEM(unit, BF16),
            pltpu.VMEM(unit, BF16),
            pltpu.VMEM((2, ROWS, 128), F32),
            pltpu.VMEM((2, ROWS, 128), F32),
            pltpu.VMEM((2, ROWS, 128), F32),
            pltpu.VMEM((ROWS, 128), F32),
            pltpu.VMEM((ROWS, 128), F32),
            pltpu.VMEM((3, ROWS, 128), F32),
            pltpu.VMEM((3, ROWS, 128), F32),
            pltpu.VMEM((ALL // 128, 4 * H, 128), F32),
            pltpu.VMEM((ALL // 128, 2 * H, 128), F32),
            pltpu.VMEM((2, 4 * H, 128), F32),
            pltpu.VMEM((2 * ROWS, 128), F32),
            pltpu.VMEM((1, CHIP), F32),
            pltpu.SMEM((1,), jnp.int32),
            dma((8,)),
            dma((4,)),
            dma((2,)),
            dma((2,)),
            dma((2, PLANE)),
            dma((2,)),
            dma((2,)),
            dma((2,)),
            dma((2,)),
            dma((2,)),
            dma((2,)),
            dma((3,)),
            dma((3,)),
            pltpu.SemaphoreType.REGULAR,
            pltpu.SemaphoreType.REGULAR,
        ],
        compiler_params=pltpu.CompilerParams(
            collective_id=0, has_side_effects=True, vmem_limit_bytes=56 * 1024 * 1024
        ),
        name="window",
    )(inputs, cotangent, weights, first_moment, second_moment, anchor, momentum, fragment)
    return pl.pallas_call(
        place_results,
        out_shape=tuple(jax.ShapeDtypeStruct(r.shape, r.dtype) for r in results),
        in_specs=[vmem] * 3,
        out_specs=(vmem,) * 3,
        name="results",
    )(*(pltpu.with_memory_space_constraint(r, pltpu.VMEM) for r in results))


def solution(mesh):
    placed = (
        P("rep", "fsdp", None),
        P("rep", "fsdp", None),
        P("rep", None, "fsdp", None),
        P("rep", None, "fsdp", None),
        P("rep", None, "fsdp", None),
        P("fsdp", None),
        P("fsdp", None),
        P(),
    )
    return jax.shard_map(
        shards,
        mesh=mesh,
        in_specs=placed,
        out_specs=(P("rep", None, "fsdp", None), P("fsdp", None), P("fsdp", None)),
        check_vma=False,
    )
```

```python
import math

import jax
import jax.numpy as jnp
from jax import lax
from jax.experimental import pallas as pl
from jax.experimental.pallas import tpu as pltpu
from jax.sharding import PartitionSpec as P

norm_eps = 1e-05
beta_one = 0.9
beta_two = 0.95
adam_eps = 1e-08
decay_rate = 0.1
inner_rate = 0.05
outer_rate = 0.7
outer_beta = 0.9
mixing = 0.5

MESH = pl.DeviceIdType.MESH
TOK = 128
D = 7168
H = 32
ROWS = 56
PLANE = 16
REPS = 8
F32 = jnp.float32
BF16 = jnp.bfloat16
CHIP = 2 * TOK
GRADS = CHIP
STACK = 2 * CHIP
ALL = STACK + 4 * H

NT = (((1,), (1,)), ((), ()))
NN = (((1,), (0,)), ((), ()))


def dot(a, b, dims):
    return lax.dot_general(a, b, dims, preferred_element_type=F32)


def kernel(
    x_h, g_h, w_h, fm_h, sm_h, an_h, mo_h, fr_h,
    new_w, new_a, new_m,
    stack, across, w_all, send, recv, z_send, z_recv, staged, w_own, fm, sm, an, mo, rep_send, rep_recv,
    proj, coef, expand, flat, ss,
    step_s, load_sem, z_sems, z_back_sems, ring_send, ring_recv, fwd_send, fwd_recv, tok_send, tok_recv,
    red_send, red_recv, rep_out, rep_in, there, ready,
):
    rep = lax.axis_index("rep")
    fsdp = lax.axis_index("fsdp")
    place = fsdp // 4
    zh = (fsdp // 2) % 2
    core = fsdp % 2

    def peer(k):
        return lax.rem(place + k, PLANE)

    def in_plane(q):
        return (rep, q * 4 + zh * 2 + core)

    early = zh == 0
    late = zh == 1
    other_z = (rep, place * 4 + (1 - zh) * 2 + core)
    sibling = (rep, place * 4 + zh * 2 + (1 - core))
    across_rep = (
        lax.rem(rep + 4, REPS),
        rep + 2 - 4 * lax.rem(rep // 2, 2),
        rep + 1 - 2 * lax.rem(rep, 2),
    )

    def remote(src, dst, ssem, rsem, device):
        return pltpu.make_async_remote_copy(
            src_ref=src, dst_ref=dst, send_sem=ssem, recv_sem=rsem, device_id=device, device_id_type=MESH
        )

    barrier = pltpu.get_barrier_semaphore()

    def greet(device):
        pl.semaphore_signal(barrier, inc=1, device_id=device, device_id_type=MESH)

    over = (rep, fsdp - core + 2 - 4 * zh)
    over_staged = (across_rep[0], fsdp - core + 2 - 4 * zh)

    @pl.when(early & (core == 0))
    def _():
        greet((across_rep[0], fsdp))
        greet(over)

    @pl.when(early & (core == 1))
    def _():
        greet((rep, fsdp + 2))

    @pl.when(early)
    def _():
        greet(over_staged)

    @pl.when(late & (core == 1))
    def _():
        greet(sibling)

    for r in across_rep:
        greet((r, place * 4 + zh * 2 + 1))

    @pl.when(core == 0)
    def _():
        greet(sibling)

    def greet_plane(k, _):
        greet((rep, peer(k) * 4 + zh * 2 + 1))
        return 0

    lax.fori_loop(1, PLANE, greet_plane, 0)

    loads = [
        pltpu.make_async_copy(src, dst, load_sem.at[i])
        for i, (src, dst) in enumerate(
            [
                (w_h.at[0], w_own),
                (x_h.at[0], stack.at[pl.ds(0, TOK)]),
                (g_h.at[0], stack.at[pl.ds(GRADS, TOK)]),
                (fm_h.at[0], fm),
                (sm_h.at[0], sm),
                (an_h, an),
                (mo_h, mo),
                (fr_h, step_s),
            ]
        )
    ]
    for load in loads:
        load.start()
    @pl.when(late & (core == 0))
    def _():
        pl.semaphore_wait(barrier, 4)
        for c in range(2):
            pl.semaphore_signal(there, inc=1, device_id=(across_rep[0], fsdp - 2 + c), device_id_type=MESH)

    loads[0].wait()
    flat[pl.ds(0, ROWS, stride=2), :] = w_own[0]
    flat[pl.ds(1, ROWS, stride=2), :] = w_own[1]
    w_all[0, 0, place] = flat[...].astype(BF16).reshape(ROWS, 2, 128)
    own = w_all.at[0, 0, place]
    z_copy = remote(own, w_all.at[1, 0, place], z_sems.at[0], z_sems.at[1], other_z)
    half = remote(own, staged, z_sems.at[2], z_sems.at[3], (across_rep[0], fsdp))
    rest = remote(staged, w_all.at[1, 0, place], z_sems.at[0], z_sems.at[1], (across_rep[0], fsdp + 2 - 4 * zh))

    @pl.when(early & (core == 0))
    def _():
        pl.semaphore_wait(barrier, 1)
        half.start()

    @pl.when(late & (core == 0))
    def _():
        z_copy.start()

    loads[7].wait()
    step = step_s[0]
    chosen = lax.rem(step, 2).astype(F32)
    loads[5].wait()
    rep_send[0] = an[...] - (w_own[0] * (1.0 - chosen) + w_own[1] * chosen)

    def turn(start):
        def one(r, _):
            at = pl.multiple_of(r * 128, 128)
            across[pl.ds(at, 128), start : start + TOK] = stack[pl.ds(start, TOK), pl.ds(at, 128)].T
            return 0

        lax.fori_loop(0, ROWS, one, 0, unroll=14)

    loads[1].wait()
    turn(0)
    loads[2].wait()
    turn(GRADS)

    @pl.when(core == 1)
    def _():
        pl.semaphore_wait(barrier, 2 * PLANE - 1 + 2 * len(across_rep) + zh)
        pl.semaphore_signal(ready, inc=1, device_id=sibling, device_id_type=MESH)

    @pl.when(core == 0)
    def _():
        pl.semaphore_wait(ready, 1)

    @pl.when(early & (core == 1))
    def _():
        half.start()

    @pl.when(late & (core == 1))
    def _():
        z_copy.start()

    def spread(h):
        def one(k, _):
            remote(
                w_all.at[h, 0, place], w_all.at[h, 0, place], ring_send.at[h], ring_recv.at[h, place], in_plane(peer(k))
            ).start()
            return 0

        lax.fori_loop(1, PLANE, one, 0)

    def hand_on(h, q):
        remote(w_all.at[h, 0, q], w_all.at[h, 1, q], fwd_send.at[h], fwd_recv.at[h], sibling).start()

    def collect(h):
        def one(k, _):
            q = lax.rem(place + PLANE - k, PLANE)
            remote(
                w_all.at[h, 0, q], w_all.at[h, 0, q], ring_send.at[h], ring_recv.at[h, q], in_plane(q)
            ).wait_recv()
            hand_on(h, q)
            return 0

        lax.fori_loop(1, PLANE, one, 0)

    @pl.when(early)
    def _():
        half.wait_recv()
        pl.semaphore_wait(there, 1)
        rest.start()

    spread(0)
    hand_on(0, place)
    tok_copies = []
    for i, start in enumerate((0, GRADS)):
        copy = remote(
            stack.at[pl.ds(start, TOK)], stack.at[pl.ds(start + TOK, TOK)], tok_send.at[i], tok_recv.at[i], sibling
        )
        tok_copies.append(copy)

    adds = [
        remote(rep_send.at[i], rep_recv.at[i], rep_out.at[i], rep_in.at[i], (across_rep[i], fsdp)) for i in range(3)
    ]

    for copy in tok_copies:
        copy.start()
    adds[0].start()

    z_copy.wait_recv()
    spread(1)
    hand_on(1, place)

    adds[0].wait_recv()
    rep_send[1] = rep_send[0] + rep_recv[0]
    adds[1].start()

    def relayout(h):
        most = w_all.at[h, 1]
        remote(most, most, fwd_send.at[h], fwd_recv.at[h], sibling).wait_recv()

        def one(r, _):
            at = pl.multiple_of(r * 128, 128)
            for c in range(2):
                stack[pl.ds(STACK + h * 64 + c * 32, 32), pl.ds(at, 128)] = w_all[h, c, :, r].reshape(32, 128)
            return 0

        lax.fori_loop(0, ROWS, one, 0, unroll=8)

    for copy, start in zip(tok_copies, (TOK, GRADS + TOK), strict=True):
        copy.wait_recv()
        turn(start)

    def square(r, acc):
        v = across[pl.ds(pl.multiple_of(r * 128, 128), 128), 0:CHIP].astype(F32)
        v = v * v
        for i in range(16):
            acc += v[i * 8 : i * 8 + 8]
        return acc

    acc = lax.fori_loop(0, ROWS, square, jnp.zeros((8, CHIP), F32), unroll=4)
    ss[...] = jnp.sum(acc, axis=0, keepdims=True)

    collect(0)
    relayout(0)
    adds[1].wait_recv()
    rep_send[2] = rep_send[1] + rep_recv[1]
    adds[2].start()
    collect(1)
    relayout(1)

    with_tokens = dot(stack[STACK:ALL, :], across[...], NN)
    for j in range(STACK // 128):
        proj[j] = with_tokens[:, j * 128 : (j + 1) * 128]
    proj[STACK // 128] = dot(stack[STACK:ALL, :], stack[STACK:ALL, :], NT)

    def rows_of(kind, layer, cols):
        return jnp.concatenate(
            [
                jnp.concatenate([proj[j, pl.ds(hc * 32 + kind * 16 + layer, 8, stride=2), :] for hc in range(4)], axis=0)
                for j in cols
            ],
            axis=1,
        )

    tokens, grads, units = (0, 1), (2, 3), (4,)
    in_scale = D ** (-0.5)
    out_scale = H ** (-0.5)

    def put(kind, layer, v):
        expand[...] = jnp.zeros_like(expand)
        for j in range(2):
            for hc in range(4):
                expand[j, pl.ds(hc * 32 + kind * 16 + layer, 8, stride=2), :] = v[
                    hc * 8 : hc * 8 + 8, j * 128 : (j + 1) * 128
                ]
        return jnp.concatenate([expand[0], expand[1]], axis=1).astype(BF16)

    ss0 = ss[...]
    inv0 = lax.rsqrt(ss0 * (1.0 / D) + norm_eps)
    pre0 = rows_of(0, 0, tokens) * (inv0 * in_scale)
    sig0 = jax.nn.sigmoid(pre0)
    act0 = pre0 * sig0 * out_scale
    out0_h = rows_of(1, 0, tokens)
    gram = jnp.concatenate([rows_of(0, 1, units), rows_of(1, 0, units)], axis=0).astype(BF16)
    act_e = put(1, 0, act0)
    mixed = dot(gram, act_e, NN)
    in1_h1 = rows_of(0, 1, tokens) + mixed[0:H]
    out0_h1 = out0_h + mixed[H : 2 * H]
    ss1 = ss0 + jnp.sum(act0 * (out0_h + out0_h1), axis=0, keepdims=True)
    inv1 = lax.rsqrt(jnp.maximum(ss1, 0.0) * (1.0 / D) + norm_eps)
    pre1 = in1_h1 * (inv1 * in_scale)
    sig1 = jax.nn.sigmoid(pre1)
    act1 = pre1 * sig1 * out_scale
    grad_pre1 = rows_of(1, 1, grads) * out_scale * sig1 * (1.0 + pre1 * (1.0 - sig1))
    back = grad_pre1 * (inv1 * in_scale)
    pull = (inv1 * inv1 * (1.0 / D)) * jnp.sum(back * in1_h1, axis=0, keepdims=True)
    back_e = put(0, 1, back)
    grad_act0 = rows_of(1, 0, grads) + dot(gram[H : 2 * H], back_e, NN) - pull * out0_h1
    grad_pre0 = grad_act0 * out_scale * sig0 * (1.0 + pre0 * (1.0 - sig0))

    act0_b = act0.astype(BF16)
    pulled = act0 * pull
    mix1 = dot(back.astype(BF16), act_e, NT)
    mix0 = dot(act0_b, back_e, NT) - dot(pulled.astype(BF16), act_e, NT)
    zero = jnp.zeros((H, CHIP), F32)
    zero_u = jnp.zeros((H, 4 * H), F32)
    for kind, layer, parts in (
        (0, 0, (grad_pre0 * (inv0 * in_scale), zero, zero_u)),
        (0, 1, (back, zero, mix1)),
        (1, 0, (-pulled, act0, mix0)),
        (1, 1, (zero, act1, zero_u)),
    ):
        for h in range(2):
            for part, cols in zip(parts, (tokens, grads, units), strict=True):
                for i, j in enumerate(cols):
                    coef[j, pl.ds(h * 32 + kind * 16 + layer, 8, stride=2), :] = part[
                        h * 16 : h * 16 + 8, i * 128 : (i + 1) * 128
                    ]

    def gradients(h):
        weights = jnp.concatenate(
            [coef[j, pl.ds(pl.multiple_of(h * 32, 32), 32), :] for j in range(ALL // 128)], axis=1
        ).astype(BF16)
        for part in range(4):
            first = part * (ROWS // 4)
            out = dot(weights, stack[:, first * 128 : (first + ROWS // 4) * 128], NN).astype(BF16)
            for j in range(ROWS // 4):
                send[h, :, first + j] = out[:, j * 128 : (j + 1) * 128].reshape(PLANE, 2, 128)
            rows = pl.ds(first, ROWS // 4)

            def out_one(k, _, rows=rows, part=part):
                q = peer(k)
                remote(
                    send.at[h, q, rows], recv.at[h, place, rows], red_send.at[h], red_recv.at[h, part // 2], in_plane(q)
                ).start()
                return 0

            lax.fori_loop(1, PLANE, out_one, 0)
        recv[h, place] = send[h, place]

    def rows_in(half):
        return pl.ds(half * (ROWS // 2), ROWS // 2)

    def summed(h, half):
        most = recv.at[h, pl.ds(0, PLANE - 1), rows_in(half)]
        pltpu.make_async_copy(most, most, red_recv.at[h, half]).wait()
        total = recv[h, 0, rows_in(half)].reshape(ROWS, 128).astype(F32)
        for q in range(1, PLANE):
            total += recv[h, q, rows_in(half)].reshape(ROWS, 128).astype(F32)
        return total

    gradients(1)

    @pl.when(early)
    def _():
        gradients(0)

    z_backs = []
    for half_at in range(2):
        z_send[rows_in(half_at)] = summed(1, half_at).astype(BF16).reshape(ROWS // 2, 2, 128)
        z_backs.append(
            remote(
                z_send.at[rows_in(half_at)], z_recv.at[rows_in(half_at)], z_back_sems.at[half_at],
                z_back_sems.at[2 + half_at], other_z,
            )
        )
        z_backs[half_at].start()

    @pl.when(late)
    def _():
        gradients(0)


    for load in (loads[3], loads[4], loads[6]):
        load.wait()
    adds[2].wait_recv()
    total = rep_send[2] + rep_recv[2]
    anchor = an[...]
    delta = total * (1.0 / REPS)
    velocity = outer_beta * mo[...] + delta
    new_anchor = anchor - outer_rate * (delta + outer_beta * velocity)
    new_m[...] = velocity
    new_a[...] = new_anchor

    count = jnp.full((8, 128), step.astype(F32), F32)
    correct_one = (1.0 - jnp.exp(count * math.log(beta_one)))[0:1]
    correct_two = (1.0 - jnp.exp(count * math.log(beta_two)))[0:1]
    for half_at in range(2):
        flat[pl.ds(half_at * ROWS, ROWS), :] = summed(0, half_at)
    for half_at in range(2):
        z_backs[half_at].wait_recv()
        there_too = z_recv[rows_in(half_at)].reshape(ROWS, 128).astype(F32)
        flat[pl.ds(half_at * ROWS, ROWS), :] = (flat[pl.ds(half_at * ROWS, ROWS), :] + there_too) * (
            1.0 / (TOK * 64)
        )
    for layer in range(2):
        gradient = flat[pl.ds(layer, ROWS, stride=2), :]
        params = w_own[layer]
        one = beta_one * fm[layer] + (1.0 - beta_one) * gradient
        two = beta_two * sm[layer] + (1.0 - beta_two) * gradient * gradient
        updated = params - inner_rate * (
            one / correct_one / (jnp.sqrt(two / correct_two) + adam_eps) + decay_rate * params
        )
        merged = mixing * updated + (1.0 - mixing) * new_anchor
        here = chosen if layer == 1 else 1.0 - chosen
        new_w[0, layer] = jnp.where(jnp.full((ROWS, 128), here, F32) > 0.5, merged, updated)

    @pl.when(early)
    def _():
        half.wait_send()

    z_copy.wait_send()
    for copy in [*z_backs, *tok_copies, *adds]:
        copy.wait_send()
    for h in range(2):
        most = w_all.at[h, 0, pl.ds(0, PLANE - 1)]
        pltpu.make_async_copy(most, most, ring_send.at[h]).wait()
        pltpu.make_async_copy(w_all.at[h, 0], w_all.at[h, 0], fwd_send.at[h]).wait()
        most = send.at[h, pl.ds(0, PLANE - 1)]
        pltpu.make_async_copy(most, most, red_send.at[h]).wait()


def place_results(a, b, c, to_a, to_b, to_c):
    to_a[...] = a[...]
    to_b[...] = b[...]
    to_c[...] = c[...]


def shards(inputs, cotangent, weights, first_moment, second_moment, anchor, momentum, fragment):
    hbm = pl.BlockSpec(memory_space=pltpu.HBM)
    vmem = pl.BlockSpec(memory_space=pltpu.VMEM)
    dma = pltpu.SemaphoreType.DMA
    unit = (ROWS, 2, 128)
    results = pl.pallas_call(
        kernel,
        out_shape=(
            pltpu.VMEM((1, 2, ROWS, 128), F32),
            pltpu.VMEM((ROWS, 128), F32),
            pltpu.VMEM((ROWS, 128), F32),
        ),
        in_specs=[hbm] * 8,
        out_specs=(vmem, vmem, vmem),
        scratch_shapes=[
            pltpu.VMEM((ALL, D), BF16),
            pltpu.VMEM((D, STACK), BF16),
            pltpu.VMEM((2, 2, PLANE) + unit, BF16),
            pltpu.VMEM((2, PLANE) + unit, BF16),
            pltpu.VMEM((2, PLANE) + unit, BF16),
            pltpu.VMEM(unit, BF16),
            pltpu.VMEM(unit, BF16),
            pltpu.VMEM(unit, BF16),
            pltpu.VMEM((2, ROWS, 128), F32),
            pltpu.VMEM((2, ROWS, 128), F32),
            pltpu.VMEM((2, ROWS, 128), F32),
            pltpu.VMEM((ROWS, 128), F32),
            pltpu.VMEM((ROWS, 128), F32),
            pltpu.VMEM((3, ROWS, 128), F32),
            pltpu.VMEM((3, ROWS, 128), F32),
            pltpu.VMEM((ALL // 128, 4 * H, 128), F32),
            pltpu.VMEM((ALL // 128, 2 * H, 128), F32),
            pltpu.VMEM((2, 4 * H, 128), F32),
            pltpu.VMEM((2 * ROWS, 128), F32),
            pltpu.VMEM((1, CHIP), F32),
            pltpu.SMEM((1,), jnp.int32),
            dma((8,)),
            dma((4,)),
            dma((4,)),
            dma((2,)),
            dma((2, PLANE)),
            dma((2,)),
            dma((2,)),
            dma((2,)),
            dma((2,)),
            dma((2,)),
            dma((2, 2)),
            dma((3,)),
            dma((3,)),
            pltpu.SemaphoreType.REGULAR,
            pltpu.SemaphoreType.REGULAR,
        ],
        compiler_params=pltpu.CompilerParams(
            collective_id=0, has_side_effects=True, vmem_limit_bytes=56 * 1024 * 1024
        ),
        name="window",
    )(inputs, cotangent, weights, first_moment, second_moment, anchor, momentum, fragment)
    return pl.pallas_call(
        place_results,
        out_shape=tuple(jax.ShapeDtypeStruct(r.shape, r.dtype) for r in results),
        in_specs=[vmem] * 3,
        out_specs=(vmem,) * 3,
        name="results",
    )(*(pltpu.with_memory_space_constraint(r, pltpu.VMEM) for r in results))


def solution(mesh):
    placed = (
        P("rep", "fsdp", None),
        P("rep", "fsdp", None),
        P("rep", None, "fsdp", None),
        P("rep", None, "fsdp", None),
        P("rep", None, "fsdp", None),
        P("fsdp", None),
        P("fsdp", None),
        P(),
    )
    return jax.shard_map(
        shards,
        mesh=mesh,
        in_specs=placed,
        out_specs=(P("rep", None, "fsdp", None), P("fsdp", None), P("fsdp", None)),
        check_vma=False,
    )
```
